32 devices in a mesh: dp: 8 (over z, y), seq: 4 (over x, core).
Axes of the slice: x: 2, y: 2, z: 4, core: 2. Of those that a mesh axis runs over, the one named last changes fastest.
Arguments:
- layer_input: bfloat16 [8, 2048, 1024], P('dp', 'seq'), may hold values from -6 to 6
- segment_length: int32 [8], P('dp'), may hold values from 1434 to 2048, as said below
- output_gradient: bfloat16 [8, 2048, 1024], P('dp', 'seq'), may hold values from -6 to 6
- state_cotangent: float32 [8, 512, 1024], P('dp'), may hold values from -6 to 6
- query_key_value_weight: bfloat16 [1024, 3072], P(('dp', 'seq')), may hold values from -0.1875 to 0.1875
- state_key_value_weight: bfloat16 [1024, 2048], P(('dp', 'seq')), may hold values from -0.1875 to 0.1875
- state_query_weight: bfloat16 [1024, 1024], P(('dp', 'seq')), may hold values from -0.1875 to 0.1875
- output_weight: bfloat16 [1024, 1024], P(('dp', 'seq')), may hold values from -0.75 to 0.75
- merge_weight: bfloat16 [1024, 1024], P(('dp', 'seq')), may hold values from -0.375 to 0.375
- up_weight: bfloat16 [1024, 4096], P(('dp', 'seq')), may hold values from -0.1875 to 0.1875
- down_weight: bfloat16 [4096, 1024], P(('dp', 'seq')), may hold values from -0.09375 to 0.09375
- initial_state_learned: bfloat16 [512, 1024], P(None, ('dp', 'seq')), may hold values from -6 to 6
- attention_norm_gain: bfloat16 [1024], P(('dp', 'seq')), may hold values from 0.5 to 1.5
- feedforward_norm_gain: bfloat16 [1024], P(('dp', 'seq')), may hold values from 0.5 to 1.5
- state_norm_gain: bfloat16 [1024], P(('dp', 'seq')), may hold values from 0.5 to 1.5
- state_gate_logits: bfloat16 [1024], P(('dp', 'seq')), may hold values from -2 to 3
- relative_position_bias: bfloat16 [256], P(('dp', 'seq')), may hold values from -5 to 5
Outputs:
- layer_out: bfloat16 [8, 2048, 1024], P('dp', 'seq')
- state_out: float32 [8, 512, 1024], P('dp', 'seq')
- x_grad: float32 [8, 2048, 1024], P('dp', 'seq')
- w_qkv_grad: float32 [1024, 3072], P(('dp', 'seq'))
- w_skv_grad: float32 [1024, 2048], P(('dp', 'seq'))
- w_query_grad: float32 [1024, 1024], P(('dp', 'seq'))
- w_out_grad: float32 [1024, 1024], P(('dp', 'seq'))
- w_merge_grad: float32 [1024, 1024], P(('dp', 'seq'))
- w_up_grad: float32 [1024, 4096], P(('dp', 'seq'))
- w_down_grad: float32 [4096, 1024], P(('dp', 'seq'))
- state_init_grad: float32 [512, 1024], P(None, ('dp', 'seq'))
- gain_attn_grad: float32 [1024], P(('dp', 'seq'))
- gain_mlp_grad: float32 [1024], P(('dp', 'seq'))
- gain_state_grad: float32 [1024], P(('dp', 'seq'))
- gate_logit_grad: float32 [1024], P(('dp', 'seq'))
- rel_bias_grad: float32 [256], P(('dp', 'seq'))
The draws below stay inside these ranges and needn't reach their ends.
Inputs may be any that keep to these rules, and one draw needn't show every extreme that they name: A segment's first segment_length tokens are valid and the rest are padding at its end. In every draw some segment is full and some has the fewest valid tokens.
All inputs are finite; a program needn't handle non-finite values.
Results may differ from the reference program's by a relative error of at most 0.025.
Values may be sent and summed in bfloat16 or wider, within the bound.
No kernel may reach another device: no remote copies, remote signals or barrier semaphores. Data moves between devices by JAX's collectives and lax.ppermute only.
A program may use at most 384 MiB of HBM per device.

```python
import jax
import jax.numpy as jnp
import numpy as np
from jax import lax

MODEL_WIDTH = 1024
HEADS = 8
HEAD = 128
FF = 4096
BLOCK = 512
STATES = 512
BUCKETS = 32
MAX_DIST = 128
SEGLEN = 2048
SEGS = 8
N_SEQ = 4


def draw_segment_length(key, part):
    low_end = SEGLEN - 3 * SEGLEN // 10
    first, second, third = jax.random.split(key, 3)
    lengths = jax.random.randint(first, (SEGS,), low_end, SEGLEN + 1)
    top_index = jax.random.randint(second, (), 0, SEGS)
    other_index = (top_index + jax.random.randint(third, (), 1, SEGS)) % SEGS
    return lengths.at[top_index].set(SEGLEN).at[other_index].set(low_end).astype(jnp.int32)


def block_levels(own_key, dims, cuts, low, high):
    def one(dim, blocks):
        heights = jax.random.uniform(jax.random.fold_in(jax.random.fold_in(own_key, 6), dim), (blocks,), jnp.float32, low / len(cuts), high / len(cuts))
        return jnp.repeat(jnp.exp(heights), dims[dim] // blocks).reshape((-1,) + (1,) * (len(dims) - dim - 1))

    loudness = one(*cuts[0])
    for cut in cuts[1:]:
        loudness = loudness * one(*cut)
    return loudness


def normal_values(key, shape, deviation, limit, cuts=(), kind=jnp.bfloat16):
    level = block_levels(key, shape, cuts, -0.22, 0.18) if cuts else 1.0
    entries = jax.random.normal(key, shape, jnp.float32) * deviation * level
    return jnp.minimum(jnp.maximum(entries, -limit), limit).astype(kind)


def setup_inputs(seed: int = 0) -> dict:
    splits = jax.random.split(jax.random.key(seed), 18)
    layer_input = normal_values(splits[0], (SEGS, SEGLEN, MODEL_WIDTH), 1.0, 6.0, ((0, 8), (1, 4)))
    segment_length = draw_segment_length(jax.random.fold_in(splits[17], 71), 0)
    output_gradient = normal_values(splits[2], (SEGS, SEGLEN, MODEL_WIDTH), 1.0, 6.0, ((0, 8), (1, 4)))
    state_cotangent = normal_values(splits[3], (SEGS, STATES, MODEL_WIDTH), 1.0, 6.0, ((0, 8),), jnp.float32)
    query_key_value_weight = normal_values(splits[4], (MODEL_WIDTH, 3 * MODEL_WIDTH), MODEL_WIDTH ** -0.5, 0.1875, ((0, 32),))
    state_key_value_weight = normal_values(splits[5], (MODEL_WIDTH, 2 * MODEL_WIDTH), MODEL_WIDTH ** -0.5, 0.1875, ((0, 32),))
    state_query_weight = normal_values(splits[6], (MODEL_WIDTH, MODEL_WIDTH), MODEL_WIDTH ** -0.5, 0.1875, ((0, 32),))
    output_weight = normal_values(splits[7], (MODEL_WIDTH, MODEL_WIDTH), (MODEL_WIDTH // 16) ** -0.5, 0.75, ((0, 32),))
    merge_weight = normal_values(splits[8], (MODEL_WIDTH, MODEL_WIDTH), (MODEL_WIDTH // 4) ** -0.5, 0.375, ((0, 32),))
    up_weight = normal_values(splits[9], (MODEL_WIDTH, FF), MODEL_WIDTH ** -0.5, 0.1875, ((0, 32),))
    down_weight = normal_values(splits[10], (FF, MODEL_WIDTH), FF ** -0.5, 0.09375, ((0, 32),))
    initial_state_learned = normal_values(splits[11], (STATES, MODEL_WIDTH), 1.0, 6.0, ((1, 32),))
    attention_norm_gain = jnp.clip(1.0 + 0.1 * jax.random.normal(splits[12], (MODEL_WIDTH,), jnp.float32), 0.5, 1.5).astype(jnp.bfloat16)
    feedforward_norm_gain = jnp.clip(1.0 + 0.1 * jax.random.normal(splits[13], (MODEL_WIDTH,), jnp.float32), 0.5, 1.5).astype(jnp.bfloat16)
    state_norm_gain = jnp.clip(1.0 + 0.1 * jax.random.normal(splits[14], (MODEL_WIDTH,), jnp.float32), 0.5, 1.5).astype(jnp.bfloat16)
    state_gate_logits = jnp.clip(-2.0 + 5.0 * jax.random.uniform(splits[15], (MODEL_WIDTH,), jnp.float32) ** block_levels(splits[15], (MODEL_WIDTH,), ((0, 32),), -0.2, 0.2), -2.0, 3.0).astype(jnp.bfloat16)
    relative_position_bias = normal_values(splits[16], (HEADS * BUCKETS,), 1.0, 5.0, ((0, 32),))
    return dict(layer_input=layer_input, segment_length=segment_length, output_gradient=output_gradient, state_cotangent=state_cotangent, query_key_value_weight=query_key_value_weight, state_key_value_weight=state_key_value_weight, state_query_weight=state_query_weight, output_weight=output_weight, merge_weight=merge_weight, up_weight=up_weight, down_weight=down_weight, initial_state_learned=initial_state_learned, attention_norm_gain=attention_norm_gain, feedforward_norm_gain=feedforward_norm_gain, state_norm_gain=state_norm_gain, state_gate_logits=state_gate_logits, relative_position_bias=relative_position_bias)


EPS = 1e-05
NEG = -1e+30
HIGH = lax.Precision.HIGHEST

@jax.custom_vjp
def low(v):
    return lax.optimization_barrier(v.astype(jnp.bfloat16)).astype(jnp.float32)

@jax.custom_vjp
def low_back(v):
    return v

def low_keep(v):
    return (low(v), None)

def low_pass(kept, grad):
    return (grad,)

def back_keep(v):
    return (v, None)

def back_low(kept, grad):
    return (low(grad),)
low.defvjp(low_keep, low_pass)
low_back.defvjp(back_keep, back_low)

def bucket_ids(length, buckets, max_dist):
    dist = np.arange(length)[:, None] - np.arange(length)[None, :]
    dist = np.maximum(dist, 0)
    exact = buckets // 2
    scaled = np.log(np.maximum(dist, exact) / exact) / np.log(max_dist / exact) * (buckets - exact)
    far = np.minimum(exact + np.floor(scaled).astype(np.int32), buckets - 1)
    return np.where(dist < exact, dist, far).astype(np.int32)

def layer_norm(value, gain):
    mean = lax.optimization_barrier(jnp.mean(value, axis=-1, keepdims=True))
    centered = value - mean
    spread = lax.optimization_barrier(jnp.mean(centered * centered, axis=-1, keepdims=True))
    return centered * lax.rsqrt(spread + EPS) * gain

def matrix_product(left, right):
    return jnp.dot(left, right, precision=HIGH, preferred_element_type=jnp.float32)

def split_heads(value):
    return value.reshape(value.shape[0], HEADS, HEAD)

def scores_of(query, keys):
    return jnp.einsum('lhe,nhe->hln', query, keys, precision=HIGH)

def mix_of(probs, values):
    return jnp.einsum('hln,nhe->lhe', probs, values, precision=HIGH)

def block_step(layer_weights, bucket, causal, carry, inputs):
    query_key_value_weight, state_key_value_weight, state_query_weight, output_weight, merge_weight, up_weight, down_weight, initial_state_learned, attention_norm_gain, feedforward_norm_gain, state_norm_gain, state_gate_logits, relative_position_bias = layer_weights
    block_tokens, block_valid = inputs
    scale = HEAD ** (-0.5)
    gate = jax.nn.sigmoid(state_gate_logits)
    normed = low(layer_norm(block_tokens, attention_norm_gain))
    qkv = low_back(matrix_product(normed, query_key_value_weight))
    query = split_heads(low(qkv[:, :MODEL_WIDTH] * scale))
    keys = split_heads(low(qkv[:, MODEL_WIDTH:2 * MODEL_WIDTH]))
    values = split_heads(low(qkv[:, 2 * MODEL_WIDTH:]))
    carried_state = low(layer_norm(carry, state_norm_gain))
    carried_key_value = low_back(matrix_product(carried_state, state_key_value_weight))
    carried_keys = split_heads(low(carried_key_value[:, :MODEL_WIDTH]))
    carried_values = split_heads(low(carried_key_value[:, MODEL_WIDTH:]))
    state_query = split_heads(low(low_back(matrix_product(carried_state, state_query_weight)) * scale))
    table = relative_position_bias.reshape(HEADS, BUCKETS)
    own = low_back(scores_of(query, keys)) + table[:, bucket]
    allowed = jnp.logical_and(causal, block_valid[None, :])
    own = jnp.where(allowed[None], own, NEG)
    other = low_back(scores_of(query, carried_keys))
    probs = low(jax.nn.softmax(jnp.concatenate([own, other], axis=-1), axis=-1))
    mixed = mix_of(probs[..., :BLOCK], values) + mix_of(probs[..., BLOCK:], carried_values)
    mixed = low(low_back(mixed.reshape(BLOCK, MODEL_WIDTH)))
    attn = low_back(matrix_product(mixed, output_weight))
    resid = block_tokens + attn
    hidden = low(layer_norm(resid, feedforward_norm_gain))
    up = low_back(matrix_product(hidden, up_weight))
    act = low(jax.nn.gelu(up, approximate=True))
    result = resid + low_back(matrix_product(act, down_weight))
    self_part = low_back(scores_of(state_query, carried_keys))
    cross_part = low_back(scores_of(state_query, keys))
    cross_part = jnp.where(block_valid[None, None, :], cross_part, NEG)
    probs_two = low(jax.nn.softmax(jnp.concatenate([self_part, cross_part], axis=-1), axis=-1))
    update = mix_of(probs_two[..., :STATES], carried_values) + mix_of(probs_two[..., STATES:], values)
    update = low(low_back(update.reshape(STATES, MODEL_WIDTH)))
    candidate = low_back(matrix_product(update, merge_weight))
    new_state = gate * carry + (1.0 - gate) * candidate
    return (new_state, result)

def reference(layer_input, segment_length, output_gradient, state_cotangent, query_key_value_weight, state_key_value_weight, state_query_weight, output_weight, merge_weight, up_weight, down_weight, initial_state_learned, attention_norm_gain, feedforward_norm_gain, state_norm_gain, state_gate_logits, relative_position_bias):
    layer_weights = tuple((tree_element.astype(jnp.float32) for tree_element in (query_key_value_weight, state_key_value_weight, state_query_weight, output_weight, merge_weight, up_weight, down_weight, initial_state_learned, attention_norm_gain, feedforward_norm_gain, state_norm_gain, state_gate_logits, relative_position_bias)))
    tokens = layer_input.astype(jnp.float32)
    bucket = bucket_ids(BLOCK, BUCKETS, MAX_DIST)
    causal = np.tril(np.ones((BLOCK, BLOCK), dtype=bool))
    valid = (jnp.arange(SEGLEN, dtype=jnp.int32)[None, :] < segment_length[:, None]).reshape(SEGS, N_SEQ, BLOCK)

    def whole(tokens, *params):

        def step(carry, inputs):
            return block_step(params, bucket, causal, carry, inputs)

        def segment(inputs):
            seg_tokens, seg_valid = inputs
            final, outs = lax.scan(jax.checkpoint(step), params[7], (seg_tokens.reshape(N_SEQ, BLOCK, MODEL_WIDTH), seg_valid))
            return (outs.reshape(SEGLEN, MODEL_WIDTH), final)
        return lax.map(segment, (tokens, valid))
    (outs, finals), pull = jax.vjp(whole, tokens, *layer_weights)
    grads = pull((output_gradient.astype(jnp.float32), state_cotangent))
    return (outs.astype(jnp.bfloat16), finals, grads[0], grads[1], grads[2], grads[3], grads[4], grads[5], grads[6], grads[7], grads[8], grads[9], grads[10], grads[11], grads[12], grads[13])
```

```python
from functools import partial

import jax
import jax.numpy as jnp
import numpy as np
from jax import lax
from jax.experimental import pallas as pl
from jax.experimental.pallas import tpu as pltpu
from jax.sharding import PartitionSpec as P

HEADS = 8
HEAD = 128
BUCKETS = 32
MAX_DIST = 128
EPS = 1e-05
NEG = -1e30
SCALE = HEAD ** (-0.5)
AXES = ("dp", "seq")
F32 = jnp.float32
BF16 = jnp.bfloat16
MIB = 1 << 20


def bucket_of(length):
    dist = np.arange(length)
    exact = BUCKETS // 2
    scaled = np.log(np.maximum(dist, exact) / exact) / np.log(MAX_DIST / exact) * (BUCKETS - exact)
    far = np.minimum(exact + np.floor(scaled).astype(np.int32), BUCKETS - 1)
    return np.where(dist < exact, dist, far).astype(np.int32)


def dot_nn(a, b):
    return jnp.dot(a, b, preferred_element_type=F32)


def dot_nt(a, b):
    return lax.dot_general(a, b, (((1,), (1,)), ((), ())), preferred_element_type=F32)


def norm_parts(x):
    mean = jnp.mean(x, axis=-1, keepdims=True)
    centered = x - mean
    spread = jnp.mean(centered * centered, axis=-1, keepdims=True)
    rstd = lax.rsqrt(spread + EPS)
    return centered * rstd, rstd


def norm_back(x, gain, dy):
    xhat, rstd = norm_parts(x)
    dyg = dy * gain
    mean_one = jnp.mean(dyg, axis=-1, keepdims=True)
    mean_two = jnp.mean(dyg * xhat, axis=-1, keepdims=True)
    return rstd * (dyg - mean_one - xhat * mean_two), dy * xhat


def row_iota(rows, cols):
    return lax.broadcasted_iota(jnp.int32, (rows, cols), 0)


def row_chunks(rows, chunk, body):
    def step(i, carry):
        body(pl.ds(pl.multiple_of(i * chunk, chunk), chunk))
        return carry

    lax.fori_loop(0, rows // chunk, step, 0)


def project_kernel(x_ref, gains_ref, w_ref, init_t_ref, qkv_ref, h1_ref, init_ref):
    i = pl.program_id(0)

    @pl.when(i == 0)
    def _():
        def chunk(rows):
            xhat, _ = norm_parts(x_ref[rows, :].astype(F32))
            h1_ref[rows, :] = (xhat * gains_ref[0:1, :]).astype(BF16)

        row_chunks(x_ref.shape[0], 64, chunk)
        init_ref[...] = init_t_ref[...].T

    acc = dot_nn(h1_ref[...], w_ref[...])
    factor = jnp.where(i < 2, SCALE, 1.0).astype(F32)
    qkv_ref[...] = (acc * factor).astype(BF16)


def project(x, gains, wa):
    rows, width = x.shape
    states = 512
    tile = 512
    return pl.pallas_call(
        project_kernel,
        grid=(3 * width // tile,),
        in_specs=[
            pl.BlockSpec((rows, width), lambda i: (0, 0)),
            pl.BlockSpec((8, width), lambda i: (0, 0)),
            pl.BlockSpec((width, tile), lambda i: (0, i)),
            pl.BlockSpec((width, states), lambda i: (0, 7 * width // states)),
        ],
        out_specs=[
            pl.BlockSpec((rows, tile), lambda i: (0, i)),
            pl.BlockSpec((rows, width), lambda i: (0, 0)),
            pl.BlockSpec((states, width), lambda i: (0, 0)),
        ],
        out_shape=[
            jax.ShapeDtypeStruct((rows, 3 * width), BF16),
            jax.ShapeDtypeStruct((rows, width), BF16),
            jax.ShapeDtypeStruct((states, width), BF16),
        ],
        compiler_params=pltpu.CompilerParams(vmem_limit_bytes=32 * MIB),
        cost_estimate=pl.CostEstimate(flops=2 * rows * width * 3 * width, bytes_accessed=12 * MIB, transcendentals=0),
        name="project",
    )(x, gains, wa, wa)


def advance_kernel(first, flags_ref, gains_ref, c_hbm, wa_hbm, qkv_hbm, *refs):
    if not first:
        refs = refs[6:]
    (new_hbm, cs_hbm, hc_hbm, ckvq_hbm, upd_hbm, z_hbm, lse_hbm) = refs[:7]
    (c_v, w_v, m_v, kv_v, hc_v, ckvq_v, upd_v, z_v, new_v, lse_v, sem) = refs[7:]
    width = c_v.shape[1]

    @pl.when(flags_ref[0] == 1)
    def _():
        c_in = pltpu.make_async_copy(c_hbm, c_v, sem.at[0])
        w_in = pltpu.make_async_copy(wa_hbm.at[:, pl.ds(3 * width, 3 * width)], w_v, sem.at[1])
        kv_in = pltpu.make_async_copy(qkv_hbm.at[:, pl.ds(width, 2 * width)], kv_v, sem.at[2])
        m_in = pltpu.make_async_copy(wa_hbm.at[:, pl.ds(6 * width, width)], m_v, sem.at[3])
        c_in.start()
        w_in.start()
        kv_in.start()
        m_in.start()
        c_in.wait()
        c_out = pltpu.make_async_copy(c_v, cs_hbm, sem.at[0])
        c_out.start()

        def norm_chunk(rows):
            xhat, _ = norm_parts(c_v[rows, :].astype(F32))
            hc_v[rows, :] = (xhat * gains_ref[2:3, :]).astype(BF16)

        row_chunks(c_v.shape[0], 64, norm_chunk)
        hc_out = pltpu.make_async_copy(hc_v, hc_hbm, sem.at[4])
        hc_out.start()
        w_in.wait()

        def column_tile(t, carry):
            cols = pl.ds(pl.multiple_of(t * 512, 512), 512)
            factor = jnp.where(t < 4, 1.0, SCALE).astype(F32)
            ckvq_v[:, cols] = (dot_nn(hc_v[...], w_v[:, cols]) * factor).astype(BF16)
            return carry

        lax.fori_loop(0, 3 * width // 512, column_tile, 0)
        ckvq_out = pltpu.make_async_copy(ckvq_v, ckvq_hbm, sem.at[1])
        ckvq_out.start()
        kv_in.wait()
        nvalid = flags_ref[1]
        keys = kv_v.shape[0]

        def head_step(h, carry):
            off = pl.multiple_of(h * HEAD, HEAD)
            ck = ckvq_v[:, pl.ds(off, HEAD)]
            cvt = ckvq_v[:, pl.ds(off + width, HEAD)].T
            k = kv_v[:, pl.ds(off, HEAD)]
            vt = kv_v[:, pl.ds(off + width, HEAD)].T
            for part in range(2):
                q = ckvq_v[part * 256 : part * 256 + 256, pl.ds(off + 2 * width, HEAD)]
                one = dot_nt(ck, q)
                two = jnp.where(row_iota(keys, 256) < nvalid, dot_nt(k, q), NEG)
                top = jnp.maximum(
                    jnp.max(one, axis=0, keepdims=True), jnp.max(two, axis=0, keepdims=True)
                )
                one = jnp.exp(one - top)
                two = jnp.exp(two - top)
                total = jnp.sum(one, axis=0, keepdims=True) + jnp.sum(two, axis=0, keepdims=True)
                mixed = dot_nn(cvt, one.astype(BF16)) + dot_nn(vt, two.astype(BF16))
                mixed = mixed * (1.0 / total)
                upd_v[part * 256 : part * 256 + 256, pl.ds(off, HEAD)] = mixed.T.astype(BF16)
                lse_v[pl.ds(h, 1), part * 256 : part * 256 + 256] = top + jnp.log(total)
            return carry

        lax.fori_loop(0, HEADS, head_step, 0)
        upd_out = pltpu.make_async_copy(upd_v, upd_hbm, sem.at[2])
        upd_out.start()
        lse_out = pltpu.make_async_copy(lse_v, lse_hbm, sem.at[5])
        lse_out.start()
        m_in.wait()

        def merge_tile(t, carry):
            cols = pl.ds(pl.multiple_of(t * 512, 512), 512)
            z_v[:, cols] = dot_nn(upd_v[...], m_v[:, cols])
            return carry

        lax.fori_loop(0, width // 512, merge_tile, 0)
        z_out = pltpu.make_async_copy(z_v, z_hbm, sem.at[6])
        z_out.start()

        def gate_chunk(rows):
            gate = gains_ref[3:4, :]
            new = gate * c_v[rows, :].astype(F32) + (1.0 - gate) * z_v[rows, :]
            new_v[rows, :] = new.astype(BF16)

        row_chunks(c_v.shape[0], 64, gate_chunk)
        new_out = pltpu.make_async_copy(new_v, new_hbm, sem.at[3])
        new_out.start()
        c_out.wait()
        hc_out.wait()
        ckvq_out.wait()
        upd_out.wait()
        lse_out.wait()
        z_out.wait()
        new_out.wait()


def advance(flags, gains, c, wa, qkv, stash):
    states, width = c.shape
    rows = qkv.shape[0]
    hbm = pl.BlockSpec(memory_space=pl.ANY)
    shapes = [
        jax.ShapeDtypeStruct((states, width), BF16),
        jax.ShapeDtypeStruct((states, width), BF16),
        jax.ShapeDtypeStruct((states, width), BF16),
        jax.ShapeDtypeStruct((states, 3 * width), BF16),
        jax.ShapeDtypeStruct((states, width), BF16),
        jax.ShapeDtypeStruct((states, width), F32),
        jax.ShapeDtypeStruct((HEADS, states), F32),
    ]
    first = stash is None
    extra = () if first else tuple(stash)
    out = pl.pallas_call(
        partial(advance_kernel, first),
        in_specs=[
            pl.BlockSpec(memory_space=pltpu.SMEM),
            pl.BlockSpec(memory_space=pltpu.VMEM),
            hbm,
            hbm,
            hbm,
        ]
        + [hbm] * len(extra),
        out_specs=[hbm] * 7,
        out_shape=shapes,
        scratch_shapes=[
            pltpu.VMEM((states, width), BF16),
            pltpu.VMEM((width, 3 * width), BF16),
            pltpu.VMEM((width, width), BF16),
            pltpu.VMEM((rows, 2 * width), BF16),
            pltpu.VMEM((states, width), BF16),
            pltpu.VMEM((states, 3 * width), BF16),
            pltpu.VMEM((states, width), BF16),
            pltpu.VMEM((states, width), F32),
            pltpu.VMEM((states, width), BF16),
            pltpu.VMEM((HEADS, states), F32),
            pltpu.SemaphoreType.DMA((7,)),
        ],
        input_output_aliases={} if first else {5 + i: 1 + i for i in range(6)},
        compiler_params=pltpu.CompilerParams(vmem_limit_bytes=44 * MIB),
        cost_estimate=pl.CostEstimate(flops=9 << 30, bytes_accessed=24 * MIB, transcendentals=4 * MIB),
        name="advance",
    )(flags, gains, c, wa, qkv, *extra)
    return out[0], out[1:]


def bias_tiles(t_row):
    spread = jnp.broadcast_to(t_row, (128, t_row.shape[1]))
    grid = pltpu.roll(spread, 0, axis=1, stride=1, stride_axis=0)
    lane = lax.broadcasted_iota(jnp.int32, (128, 128), 1)
    sub = lax.broadcasted_iota(jnp.int32, (128, 128), 0)
    tiles = [grid[:, 128 * d : 128 * d + 128] for d in range(4)]
    tiles[0] = jnp.where(lane >= sub, tiles[0], NEG)
    return tiles


def bias_part(tiles, part):
    none = jnp.full((128, 128), NEG, F32)
    rows = []
    for j in range(2 * part + 2):
        row = [tiles[i - j] if i >= j else none for i in (2 * part, 2 * part + 1)]
        rows.append(jnp.concatenate(row, axis=1))
    return jnp.concatenate(rows, axis=0)


def own_scores(k, q, tiles, part, nvalid):
    used = 256 * (part + 1)
    scores = dot_nt(k[:used], q) + bias_part(tiles, part)
    return jnp.where(row_iota(used, 256) < nvalid, scores, NEG)


def token_kernel(flags_ref, t_ref, gains_ref, x_ref, q_ref, k_ref, v_ref, ck_ref, cv_ref, w_ref,
                 o_ref, lse_ref, x1_ref, h2_ref, acc_ref):
    i = pl.program_id(0)
    nvalid = flags_ref[1]
    for sub in range(2):
        cols = slice(sub * HEAD, sub * HEAD + HEAD)
        h = 2 * i + sub
        tiles = bias_tiles(t_ref[pl.ds(h, 1), :])
        k = k_ref[:, cols]
        vt = v_ref[:, cols].T
        ck = ck_ref[:, cols]
        cvt = cv_ref[:, cols].T
        for part in range(2):
            q = q_ref[part * 256 : part * 256 + 256, cols]
            one = dot_nt(ck, q)
            two = own_scores(k, q, tiles, part, nvalid)
            top = jnp.maximum(
                jnp.max(one, axis=0, keepdims=True), jnp.max(two, axis=0, keepdims=True)
            )
            one = jnp.exp(one - top)
            two = jnp.exp(two - top)
            total = jnp.sum(one, axis=0, keepdims=True) + jnp.sum(two, axis=0, keepdims=True)
            used = 256 * (part + 1)
            mixed = dot_nn(cvt, one.astype(BF16)) + dot_nn(vt[:, :used], two.astype(BF16))
            mixed = mixed * (1.0 / total)
            o_ref[part * 256 : part * 256 + 256, cols] = mixed.T.astype(BF16)
            lse_ref[pl.ds(h, 1), part * 256 : part * 256 + 256] = top + jnp.log(total)
    term = dot_nn(o_ref[...], w_ref[...])

    @pl.when(i == 0)
    def _():
        acc_ref[...] = x_ref[...].astype(F32) + term

    @pl.when(i > 0)
    def _():
        acc_ref[...] += term

    @pl.when(i == pl.num_programs(0) - 1)
    def _():
        def chunk(rows):
            x1 = acc_ref[rows, :]
            x1_ref[rows, :] = x1
            xhat, _ = norm_parts(x1)
            h2_ref[rows, :] = (xhat * gains_ref[1:2, :]).astype(BF16)

        row_chunks(acc_ref.shape[0], 64, chunk)


def token_forward(flags, t, gains, x, qkv, ckvq, wb):
    rows, width = x.shape
    states = ckvq.shape[0]
    steps = HEADS // 2
    return pl.pallas_call(
        token_kernel,
        grid=(steps,),
        in_specs=[
            pl.BlockSpec(memory_space=pltpu.SMEM),
            pl.BlockSpec((HEADS, rows), lambda i: (0, 0)),
            pl.BlockSpec((8, width), lambda i: (0, 0)),
            pl.BlockSpec((rows, width), lambda i: (0, 0)),
            pl.BlockSpec((rows, 256), lambda i: (0, i)),
            pl.BlockSpec((rows, 256), lambda i: (0, 4 + i)),
            pl.BlockSpec((rows, 256), lambda i: (0, 8 + i)),
            pl.BlockSpec((states, 256), lambda i: (0, i)),
            pl.BlockSpec((states, 256), lambda i: (0, 4 + i)),
            pl.BlockSpec((256, width), lambda i: (i, 0)),
        ],
        out_specs=[
            pl.BlockSpec((rows, 256), lambda i: (0, i)),
            pl.BlockSpec((HEADS, rows), lambda i: (0, 0)),
            pl.BlockSpec((rows, width), lambda i: (0, 0)),
            pl.BlockSpec((rows, width), lambda i: (0, 0)),
        ],
        out_shape=[
            jax.ShapeDtypeStruct((rows, width), BF16),
            jax.ShapeDtypeStruct((HEADS, rows), F32),
            jax.ShapeDtypeStruct((rows, width), F32),
            jax.ShapeDtypeStruct((rows, width), BF16),
        ],
        scratch_shapes=[pltpu.VMEM((rows, width), F32)],
        compiler_params=pltpu.CompilerParams(vmem_limit_bytes=40 * MIB),
        cost_estimate=pl.CostEstimate(flops=4 << 30, bytes_accessed=12 * MIB, transcendentals=4 * MIB),
        name="token_forward",
    )(flags, t, gains, x, qkv, qkv, qkv, ckvq, ckvq, wb)


def ffn_kernel(gains_ref, h2_ref, g_ref, x1_ref, wu_ref, wd_ref, wo_ref,
               act_ref, dup_ref, out_ref, dx1_ref, da_ref, do_ref, sums_ref, acc_ref, dh_ref):
    i = pl.program_id(0)
    up = dot_nn(h2_ref[...], wu_ref[...])
    dact = dot_nt(g_ref[...], wd_ref[...])
    cubic = 0.7978845608028654
    square = up * up
    th = jnp.tanh(cubic * up * (1.0 + 0.044715 * square))
    half = 0.5 * (1.0 + th)
    act = (up * half).astype(BF16)
    slope = half + (0.5 * cubic) * up * (1.0 - th * th) * (1.0 + (3 * 0.044715) * square)
    dup = (dact * slope).astype(BF16)
    act_ref[...] = act
    dup_ref[...] = dup
    out_term = dot_nn(act, wd_ref[...])
    dh_term = dot_nt(dup, wu_ref[...])

    @pl.when(i == 0)
    def _():
        acc_ref[...] = x1_ref[...] + out_term
        dh_ref[...] = dh_term

    @pl.when(i > 0)
    def _():
        acc_ref[...] += out_term
        dh_ref[...] += dh_term

    @pl.when(i == pl.num_programs(0) - 1)
    def _():
        sums_ref[...] = jnp.zeros_like(sums_ref)

        def chunk(rows):
            out_ref[rows, :] = acc_ref[rows, :].astype(BF16)
            dx, gain_term = norm_back(x1_ref[rows, :], gains_ref[1:2, :], dh_ref[rows, :])
            dx = dx + g_ref[rows, :].astype(F32)
            dx1_ref[rows, :] = dx
            da_ref[rows, :] = dx.astype(BF16)
            sums_ref[0:1, :] += jnp.sum(gain_term, axis=0, keepdims=True)

        row_chunks(acc_ref.shape[0], 64, chunk)
        do_ref[...] = dot_nt(da_ref[...], wo_ref[...]).astype(BF16)


def feed_forward(gains, h2, g, x1, wb):
    rows, width = h2.shape
    hidden = 4 * width
    tile = 512
    whole = lambda i: (0, 0)
    return pl.pallas_call(
        ffn_kernel,
        grid=(hidden // tile,),
        in_specs=[
            pl.BlockSpec((8, width), whole),
            pl.BlockSpec((rows, width), whole),
            pl.BlockSpec((rows, width), whole),
            pl.BlockSpec((rows, width), whole),
            pl.BlockSpec((width, tile), lambda i: (0, 2 + i)),
            pl.BlockSpec((tile, width), lambda i: (i % 2, 5 + i // 2)),
            pl.BlockSpec((width, width), whole),
        ],
        out_specs=[
            pl.BlockSpec((rows, tile), lambda i: (0, i)),
            pl.BlockSpec((rows, tile), lambda i: (0, i)),
            pl.BlockSpec((rows, width), whole),
            pl.BlockSpec((rows, width), whole),
            pl.BlockSpec((rows, width), whole),
            pl.BlockSpec((rows, width), whole),
            pl.BlockSpec((8, width), whole),
        ],
        out_shape=[
            jax.ShapeDtypeStruct((rows, hidden), BF16),
            jax.ShapeDtypeStruct((rows, hidden), BF16),
            jax.ShapeDtypeStruct((rows, width), BF16),
            jax.ShapeDtypeStruct((rows, width), F32),
            jax.ShapeDtypeStruct((rows, width), BF16),
            jax.ShapeDtypeStruct((rows, width), BF16),
            jax.ShapeDtypeStruct((8, width), F32),
        ],
        scratch_shapes=[pltpu.VMEM((rows, width), F32), pltpu.VMEM((rows, width), F32)],
        compiler_params=pltpu.CompilerParams(vmem_limit_bytes=52 * MIB),
        cost_estimate=pl.CostEstimate(flops=18 << 30, bytes_accessed=32 * MIB, transcendentals=2 * MIB),
        name="feed_forward",
    )(gains, h2, g, x1, wb, wb, wb)


def token_back_kernel(flags_ref, t_ref, lse_ref, q_ref, k_ref, v_ref, ck_ref, cv_ref, do_ref,
                      dq_ref, dkv_ref, dst_ref, db_ref):
    h = pl.program_id(0)
    nvalid = flags_ref[1]
    tiles = bias_tiles(t_ref[pl.ds(h, 1), :])
    k, v, ck, cv = k_ref[...], v_ref[...], ck_ref[...], cv_ref[...]
    kt, ckt = k.T, ck.T
    dk, dv, dck, dcv = [], [], [], []
    shear = [jnp.zeros((128, 128), F32) for _ in range(4)]
    for part in range(2):
        span = slice(part * 256, part * 256 + 256)
        used = 256 * (part + 1)
        q, do = q_ref[span, :], do_ref[span, :]
        lse = lse_ref[pl.ds(h, 1), span]
        one = jnp.exp(dot_nt(ck, q) - lse)
        two = jnp.exp(own_scores(k, q, tiles, part, nvalid) - lse)
        done = dot_nt(cv, do)
        dtwo = dot_nt(v[:used], do)
        inner = jnp.sum(one * done, axis=0, keepdims=True) + jnp.sum(
            two * dtwo, axis=0, keepdims=True
        )
        dcv.append(dot_nn(one.astype(BF16), do))
        dv.append(dot_nn(two.astype(BF16), do))
        one = one * (done - inner)
        two = two * (dtwo - inner)
        for j in range(2 * part + 2):
            for i in (0, 1):
                d = 2 * part + i - j
                if d >= 0:
                    shear[d] += two[128 * j : 128 * j + 128, 128 * i : 128 * i + 128]
        one, two = one.astype(BF16), two.astype(BF16)
        dck.append(dot_nn(one, q))
        dk.append(dot_nn(two, q))
        dqt = dot_nn(ckt, one) + dot_nn(kt[:, :used], two)
        dq_ref[span, :] = (dqt.T * SCALE).astype(BF16)
    for slot, pieces in ((0, dk), (1, dv)):
        dkv_ref[slot, :256, :] = (pieces[0] + pieces[1][:256]).astype(BF16)
        dkv_ref[slot, 256:, :] = pieces[1][256:].astype(BF16)
    dst_ref[0] = (dck[0] + dck[1]).astype(BF16)
    dst_ref[1] = (dcv[0] + dcv[1]).astype(BF16)
    grid = jnp.concatenate(shear, axis=1)
    size = grid.shape[1]
    flipped = grid[:8]
    for group in range(1, 16):
        flipped += pltpu.roll(grid[8 * group : 8 * group + 8], size - 8 * group, axis=1)
    for step in (1, 2, 4):
        moved = pltpu.roll(flipped, size - step, axis=1)
        flipped = jnp.where((row_iota(8, size) // step) % 2 == 1, moved, flipped)
    db_ref[pl.ds(h, 1), :] = jnp.sum(flipped, axis=0, keepdims=True)


def token_back(flags, t, lse, qkv, ckvq, do):
    rows = do.shape[0]
    width = do.shape[1]
    states = ckvq.shape[0]
    column = lambda base: (lambda h: (0, base + h))
    return pl.pallas_call(
        token_back_kernel,
        grid=(HEADS,),
        in_specs=[
            pl.BlockSpec(memory_space=pltpu.SMEM),
            pl.BlockSpec((HEADS, rows), lambda h: (0, 0)),
            pl.BlockSpec((HEADS, rows), lambda h: (0, 0)),
            pl.BlockSpec((rows, HEAD), column(0)),
            pl.BlockSpec((rows, HEAD), column(8)),
            pl.BlockSpec((rows, HEAD), column(16)),
            pl.BlockSpec((states, HEAD), column(0)),
            pl.BlockSpec((states, HEAD), column(8)),
            pl.BlockSpec((rows, HEAD), column(0)),
        ],
        out_specs=[
            pl.BlockSpec((rows, HEAD), column(0)),
            pl.BlockSpec((2, rows, HEAD), lambda h: (0, 0, h)),
            pl.BlockSpec((2, states, HEAD), lambda h: (0, 0, h)),
            pl.BlockSpec((HEADS, rows), lambda h: (0, 0)),
        ],
        out_shape=[
            jax.ShapeDtypeStruct((rows, width), BF16),
            jax.ShapeDtypeStruct((2, rows, width), BF16),
            jax.ShapeDtypeStruct((2, states, width), BF16),
            jax.ShapeDtypeStruct((HEADS, rows), F32),
        ],
        compiler_params=pltpu.CompilerParams(vmem_limit_bytes=40 * MIB),
        cost_estimate=pl.CostEstimate(flops=5 << 30, bytes_accessed=12 * MIB, transcendentals=4 * MIB),
        name="token_back",
    )(flags, t, lse, qkv, qkv, qkv, ckvq, ckvq, do)


def retreat_kernel(first, flags_ref, gains_ref, lam_hbm, wa_hbm, qkv_hbm, cs_hbm, ckvq_hbm, z_hbm,
                   lse_hbm, dst_hbm, *refs):
    if not first:
        refs = refs[4:]
    (prev_hbm, dz_hbm, dcs_hbm, dkv_hbm, sums_hbm) = refs[:5]
    (lam_v, w_v, m_v, kv_v, c_v, ckvq_v, z_v, lse_v, dst_v,
     dz_v, du_v, dcs_v, dkv_v, dh_v, prev_v, sums_v, sem) = refs[5:]
    states, width = c_v.shape

    @pl.when(flags_ref[0] == 1)
    def _():
        copies = [
            pltpu.make_async_copy(src, dst, sem.at[n])
            for n, (src, dst) in enumerate(
                (
                    (lam_hbm, lam_v),
                    (cs_hbm, c_v),
                    (z_hbm, z_v),
                    (wa_hbm.at[:, pl.ds(6 * width, width)], m_v),
                    (ckvq_hbm, ckvq_v),
                    (qkv_hbm.at[:, pl.ds(width, 2 * width)], kv_v),
                    (lse_hbm, lse_v),
                    (dst_hbm, dst_v),
                    (wa_hbm.at[:, pl.ds(3 * width, 3 * width)], w_v),
                )
            )
        ]
        for copy in copies:
            copy.start()
        for copy in copies[:3]:
            copy.wait()
        sums_v[...] = jnp.zeros_like(sums_v)

        def gate_chunk(rows):
            lam = lam_v[rows, :].astype(F32)
            dz_v[rows, :] = ((1.0 - gains_ref[3:4, :]) * lam).astype(BF16)
            change = lam * (c_v[rows, :].astype(F32) - z_v[rows, :])
            sums_v[1:2, :] += jnp.sum(change, axis=0, keepdims=True)

        row_chunks(states, 64, gate_chunk)
        dz_out = pltpu.make_async_copy(dz_v, dz_hbm, sem.at[0])
        dz_out.start()
        copies[3].wait()

        def merge_tile(t, carry):
            cols = pl.ds(pl.multiple_of(t * 512, 512), 512)
            du_v[:, cols] = dot_nt(dz_v[...], m_v[cols, :]).astype(BF16)
            return carry

        lax.fori_loop(0, width // 512, merge_tile, 0)
        for copy in copies[4:8]:
            copy.wait()
        nvalid = flags_ref[1]
        keys = kv_v.shape[0]

        def head_step(h, carry):
            off = pl.multiple_of(h * HEAD, HEAD)
            here = pl.ds(off, HEAD)
            there = pl.ds(off + width, HEAD)
            ck, cv = ckvq_v[:, here], ckvq_v[:, there]
            k, v = kv_v[:, here], kv_v[:, there]
            ckt, kt = ck.T, k.T
            total = None
            for part in range(2):
                span = slice(part * 256, part * 256 + 256)
                q = ckvq_v[span, pl.ds(off + 2 * width, HEAD)]
                du = du_v[span, here]
                lse = lse_v[pl.ds(h, 1), span]
                one = jnp.exp(dot_nt(ck, q) - lse)
                two = jnp.where(row_iota(keys, 256) < nvalid, dot_nt(k, q), NEG)
                two = jnp.exp(two - lse)
                done = dot_nt(cv, du)
                dtwo = dot_nt(v, du)
                inner = jnp.sum(one * done, axis=0, keepdims=True) + jnp.sum(
                    two * dtwo, axis=0, keepdims=True
                )
                terms = [dot_nn(one.astype(BF16), du), dot_nn(two.astype(BF16), du)]
                one = (one * (done - inner)).astype(BF16)
                two = (two * (dtwo - inner)).astype(BF16)
                terms += [dot_nn(one, q), dot_nn(two, q)]
                dqt = dot_nn(ckt, one) + dot_nn(kt, two)
                dcs_v[span, pl.ds(off + 2 * width, HEAD)] = (dqt.T * SCALE).astype(BF16)
                total = terms if total is None else [a + b for a, b in zip(total, terms)]
            dcs_v[:, there] = (total[0] + dst_v[1, :, here].astype(F32)).astype(BF16)
            dcs_v[:, here] = (total[2] + dst_v[0, :, here].astype(F32)).astype(BF16)
            dkv_v[:, there] = total[1].astype(BF16)
            dkv_v[:, here] = total[3].astype(BF16)
            return carry

        lax.fori_loop(0, HEADS, head_step, 0)
        dcs_out = pltpu.make_async_copy(dcs_v, dcs_hbm, sem.at[1])
        dcs_out.start()
        dkv_out = pltpu.make_async_copy(dkv_v, dkv_hbm, sem.at[2])
        dkv_out.start()
        copies[8].wait()
        dh_v[...] = dot_nt(dcs_v[:, :512], w_v[:, :512])

        def depth_tile(t, carry):
            cols = pl.ds(pl.multiple_of(t * 512, 512), 512)
            dh_v[...] += dot_nt(dcs_v[:, cols], w_v[:, cols])
            return carry

        lax.fori_loop(1, 3 * width // 512, depth_tile, 0)

        def norm_chunk(rows):
            dx, gain_term = norm_back(
                c_v[rows, :].astype(F32), gains_ref[2:3, :], dh_v[rows, :]
            )
            prev = dx + gains_ref[3:4, :] * lam_v[rows, :].astype(F32)
            prev_v[rows, :] = prev.astype(BF16)
            sums_v[0:1, :] += jnp.sum(gain_term, axis=0, keepdims=True)

        row_chunks(states, 64, norm_chunk)
        prev_out = pltpu.make_async_copy(prev_v, prev_hbm, sem.at[3])
        prev_out.start()
        sums_out = pltpu.make_async_copy(sums_v, sums_hbm, sem.at[4])
        sums_out.start()
        dz_out.wait()
        dcs_out.wait()
        dkv_out.wait()
        prev_out.wait()
        sums_out.wait()


def retreat(flags, gains, lam, wa, qkv, cs, ckvq, z, lse, dst, stash):
    states, width = cs.shape
    rows = qkv.shape[0]
    hbm = pl.BlockSpec(memory_space=pl.ANY)
    shapes = [
        jax.ShapeDtypeStruct((states, width), BF16),
        jax.ShapeDtypeStruct((states, width), BF16),
        jax.ShapeDtypeStruct((states, 3 * width), BF16),
        jax.ShapeDtypeStruct((rows, 2 * width), BF16),
        jax.ShapeDtypeStruct((8, width), F32),
    ]
    first = stash is None
    extra = () if first else tuple(stash)
    out = pl.pallas_call(
        partial(retreat_kernel, first),
        in_specs=[
            pl.BlockSpec(memory_space=pltpu.SMEM),
            pl.BlockSpec(memory_space=pltpu.VMEM),
        ]
        + [hbm] * (8 + len(extra)),
        out_specs=[hbm] * 5,
        out_shape=shapes,
        scratch_shapes=[
            pltpu.VMEM((states, width), lam.dtype),
            pltpu.VMEM((width, 3 * width), BF16),
            pltpu.VMEM((width, width), BF16),
            pltpu.VMEM((rows, 2 * width), BF16),
            pltpu.VMEM((states, width), BF16),
            pltpu.VMEM((states, 3 * width), BF16),
            pltpu.VMEM((states, width), F32),
            pltpu.VMEM((HEADS, states), F32),
            pltpu.VMEM((2, states, width), BF16),
            pltpu.VMEM((states, width), BF16),
            pltpu.VMEM((states, width), BF16),
            pltpu.VMEM((states, 3 * width), BF16),
            pltpu.VMEM((rows, 2 * width), BF16),
            pltpu.VMEM((states, width), F32),
            pltpu.VMEM((states, width), BF16),
            pltpu.VMEM((8, width), F32),
            pltpu.SemaphoreType.DMA((9,)),
        ],
        input_output_aliases={} if first else {10 + i: 1 + i for i in range(4)},
        compiler_params=pltpu.CompilerParams(vmem_limit_bytes=52 * MIB),
        cost_estimate=pl.CostEstimate(flops=13 << 30, bytes_accessed=32 * MIB, transcendentals=4 * MIB),
        name="retreat",
    )(flags, gains, lam, wa, qkv, cs, ckvq, z, lse, dst, *extra)
    return out[0], out[1:]


def input_grad_kernel(gains_ref, x_ref, dx1_ref, d_ref, w_ref, out_ref, sums_ref, acc_ref):
    i = pl.program_id(0)
    term = dot_nt(d_ref[...], w_ref[...])

    @pl.when(i == 0)
    def _():
        acc_ref[...] = term

    @pl.when(i > 0)
    def _():
        acc_ref[...] += term

    @pl.when(i == pl.num_programs(0) - 1)
    def _():
        sums_ref[...] = jnp.zeros_like(sums_ref)

        def chunk(rows):
            dx, gain_term = norm_back(x_ref[rows, :].astype(F32), gains_ref[0:1, :], acc_ref[rows, :])
            out_ref[rows, :] = dx1_ref[rows, :] + dx
            sums_ref[0:1, :] += jnp.sum(gain_term, axis=0, keepdims=True)

        row_chunks(acc_ref.shape[0], 64, chunk)


def input_grad(gains, x, dx1, dqkv, wa):
    rows, width = x.shape
    tile = 512
    whole = lambda i: (0, 0)
    return pl.pallas_call(
        input_grad_kernel,
        grid=(3 * width // tile,),
        in_specs=[
            pl.BlockSpec((8, width), whole),
            pl.BlockSpec((rows, width), whole),
            pl.BlockSpec((rows, width), whole),
            pl.BlockSpec((rows, tile), lambda i: (0, i)),
            pl.BlockSpec((width, tile), lambda i: (0, i)),
        ],
        out_specs=[pl.BlockSpec((rows, width), whole), pl.BlockSpec((8, width), whole)],
        out_shape=[
            jax.ShapeDtypeStruct((rows, width), F32),
            jax.ShapeDtypeStruct((8, width), F32),
        ],
        scratch_shapes=[pltpu.VMEM((rows, width), F32)],
        compiler_params=pltpu.CompilerParams(vmem_limit_bytes=40 * MIB),
        cost_estimate=pl.CostEstimate(flops=3 << 30, bytes_accessed=16 * MIB, transcendentals=0),
        name="input_grad",
    )(gains, x, dx1, dqkv, wa)


def outer_kernel(a_ref, b_ref, o_ref, at_ref):
    @pl.when(pl.program_id(1) == 0)
    def _():
        at_ref[...] = a_ref[...].T

    o_ref[...] = dot_nn(at_ref[...], b_ref[...]).astype(BF16)


def outer_product(a, b):
    rows, width = b.shape[0], 1024
    slabs = a.shape[1] // width
    tile = 512
    tiles = b.shape[1] // tile
    return pl.pallas_call(
        outer_kernel,
        grid=(slabs, tiles),
        in_specs=[
            pl.BlockSpec((rows, width), lambda s, i: (0, s)),
            pl.BlockSpec((rows, tile), lambda s, i: (0, i)),
        ],
        out_specs=pl.BlockSpec((width, tile), lambda s, i: (0, s * tiles + i)),
        out_shape=jax.ShapeDtypeStruct((width, slabs * b.shape[1]), BF16),
        scratch_shapes=[pltpu.VMEM((width, rows), BF16)],
        compiler_params=pltpu.CompilerParams(vmem_limit_bytes=32 * MIB),
        cost_estimate=pl.CostEstimate(
            flops=2 * rows * width * slabs * b.shape[1], bytes_accessed=4 * width * slabs * b.shape[1], transcendentals=0
        ),
        name="weight_grad",
    )(a, b)


def scatter_order(devices):
    bits = [1 << n for n in range(devices.bit_length() - 1)]
    rest = bits[1:]
    if len(rest) < 4:
        return [bits] * 3
    return [
        bits[:1] + rest,
        bits[:1] + rest[1:] + rest[:1],
        bits[:1] + rest[2:] + rest[:2],
    ]


def scatter_sum(value, order, devices):
    me = lax.axis_index(AXES)
    value = value.reshape(devices, value.shape[0] // devices, value.shape[1])
    left = sorted(order)
    for bit in order:
        place = left.index(bit)
        left.remove(bit)
        blocks, rows, cols = value.shape
        low = 1 << place
        view = value.reshape(blocks // (2 * low), 2, low, rows, cols)
        mine = (me // bit) % 2
        keep = lax.dynamic_index_in_dim(view, mine, 1, keepdims=False)
        send = lax.dynamic_index_in_dim(view, 1 - mine, 1, keepdims=False)
        keep = keep.reshape(blocks // 2, rows, cols)
        send = send.reshape(blocks // 2, rows, cols)
        route = [(i, i ^ bit) for i in range(devices)]
        got = lax.ppermute(send, AXES, route)
        value = keep.astype(F32) + got.astype(F32)
        if left:
            value = value.astype(BF16)
    return value[0]


def body(
    layer_input,
    segment_length,
    output_gradient,
    state_cotangent,
    query_key_value_weight,
    state_key_value_weight,
    state_query_weight,
    output_weight,
    merge_weight,
    up_weight,
    down_weight,
    initial_state_learned,
    attention_norm_gain,
    feedforward_norm_gain,
    state_norm_gain,
    state_gate_logits,
    relative_position_bias,
):
    _, rows, width = layer_input.shape
    place = lax.axis_index("seq")
    count = lax.axis_size("seq")
    devices = count * lax.axis_size("dp")
    share = width // devices
    pairs = lax.axis_size("dp")

    bias_local = relative_position_bias.shape[0]
    small = jnp.stack(
        [
            attention_norm_gain,
            feedforward_norm_gain,
            state_norm_gain,
            state_gate_logits,
            jnp.pad(relative_position_bias, (0, share - bias_local)),
        ],
        axis=1,
    )
    small = jnp.pad(small, ((0, 0), (0, 123)))
    wa = jnp.concatenate(
        [
            query_key_value_weight,
            state_key_value_weight,
            state_query_weight,
            merge_weight,
            initial_state_learned.T,
            small,
        ],
        axis=1,
    )
    up_local = up_weight.reshape(share, devices, 4, share).transpose(0, 2, 1, 3)
    down_local = down_weight.reshape(4, share, width).transpose(1, 0, 2)
    wb = jnp.concatenate(
        [output_weight, up_local.reshape(share, 4 * width), down_local.reshape(share, 4 * width)],
        axis=1,
    )
    wa = lax.all_gather(wa, AXES, axis=0, tiled=True)
    wb = lax.all_gather(wb, AXES, axis=0, tiled=True)

    vectors = wa[:, 15 * width // 2 : 15 * width // 2 + 5].astype(F32).T
    gate = jax.nn.sigmoid(vectors[3:4])
    gains = jnp.concatenate([vectors[:3], gate, jnp.zeros((4, width), F32)], axis=0)
    table = vectors[4].reshape(devices, share)[:, :bias_local].reshape(HEADS, BUCKETS)
    onehot = np.eye(BUCKETS, dtype=np.float32)[:, bucket_of(rows)]
    t = jnp.dot(table, jnp.asarray(onehot), precision=lax.Precision.HIGHEST)

    x = layer_input.reshape(rows, width)
    g = output_gradient.reshape(rows, width)
    nvalid = jnp.clip(segment_length[0] - place * rows, 0, rows).astype(jnp.int32)

    def flags(section):
        return jnp.stack([(place == section).astype(jnp.int32), nvalid])

    def hop(value, frm, to):
        route = [(d * count + frm, d * count + to) for d in range(pairs)]
        return lax.ppermute(value, AXES, route)

    qkv, h1, carry = project(x, gains, wa)
    stash = None
    for section in range(count):
        new, stash = advance(flags(section), gains, carry, wa, qkv, stash)
        if section + 1 < count:
            carry = hop(new, section, section + 1)
    cs, hc, ckvq, upd, z, lse_two = stash

    o, lse, x1, h2 = token_forward(flags(0), t, gains, x, qkv, ckvq, wb)
    act, dup, layer_out, dx1, da, do, sums_mlp = feed_forward(gains, h2, g, x1, wb)
    dq, dkv, dst, dbias = token_back(flags(0), t, lse, qkv, ckvq, do)

    back = None
    lam = state_cotangent.reshape(state_cotangent.shape[1:])
    for section in reversed(range(count)):
        prev, back = retreat(
            flags(section), gains, lam, wa, qkv, cs, ckvq, z, lse_two, dst, back
        )
        if section > 0:
            lam = hop(prev, section, section - 1)
    dz, dcs, dkv_two, sums_state = back

    quarter = new.shape[0] // count
    state_out = lax.dynamic_slice_in_dim(new, place * quarter, quarter, 0)
    for to in range(count - 1):
        got = hop(new[to * quarter : (to + 1) * quarter], count - 1, to)
        state_out = jnp.where(place == to, got, state_out)
    state_out = state_out.astype(F32)[None]

    up_grad = outer_product(h2, dup)
    down_grad = outer_product(act, g)
    out_grad = outer_product(o, da)
    early = jnp.concatenate([out_grad, up_grad, down_grad], axis=1)
    early = lax.psum_scatter(early, AXES, scatter_dimension=0, tiled=True).astype(F32)

    dqkv = jnp.concatenate(
        [
            dq,
            (dkv[0].astype(F32) + dkv_two[:, :width].astype(F32)).astype(BF16),
            (dkv[1].astype(F32) + dkv_two[:, width:].astype(F32)).astype(BF16),
        ],
        axis=1,
    )
    merge_grad = outer_product(upd, dz)
    state_grad = outer_product(hc, dcs)
    qkv_grad = outer_product(h1, dqkv)
    x_grad, sums_attn = input_grad(gains, x, dx1, dqkv, wa)
    x_grad = x_grad[None]

    init_grad = jnp.where(place == 0, prev, jnp.zeros_like(prev)).T
    buckets = jnp.asarray(np.ascontiguousarray(onehot.T))
    dtable = jnp.dot(dbias, buckets, precision=lax.Precision.HIGHEST).reshape(devices, bias_local)
    dtable = jnp.pad(dtable, ((0, 0), (0, share - bias_local))).reshape(width)
    gate_grad = sums_state[1] * gate[0] * (1.0 - gate[0])
    vector_grads = jnp.stack([sums_attn[0], sums_mlp[0], sums_state[0], gate_grad, dtable], axis=1)
    vector_grads = jnp.pad(vector_grads, ((0, 0), (0, 123))).astype(BF16)

    orders = scatter_order(devices)
    one = scatter_sum(jnp.concatenate([merge_grad, init_grad, vector_grads], axis=1), orders[0], devices)
    two = scatter_sum(state_grad, orders[1], devices)
    three = scatter_sum(qkv_grad, orders[2], devices)

    up_shard = early[:, width : 5 * width].reshape(share, 4, devices, share)
    up_shard = up_shard.transpose(0, 2, 1, 3).reshape(share, 4 * width)
    down_shard = early[:, 5 * width :].reshape(share, 4, width).transpose(1, 0, 2)
    states = width // 2
    vec = one[:, width + states :]
    return (
        layer_out[None],
        state_out,
        x_grad,
        three,
        two[:, : 2 * width],
        two[:, 2 * width :],
        early[:, :width],
        one[:, :width],
        up_shard,
        down_shard.reshape(4 * share, width),
        one[:, width : width + states].T,
        vec[:, 0],
        vec[:, 1],
        vec[:, 2],
        vec[:, 3],
        vec[:bias_local, 4],
    )


def solution(mesh):
    return jax.shard_map(
        body,
        mesh=mesh,
        in_specs=(
            P("dp", "seq", None),
            P("dp"),
            P("dp", "seq", None),
            P("dp", None, None),
            P(AXES, None),
            P(AXES, None),
            P(AXES, None),
            P(AXES, None),
            P(AXES, None),
            P(AXES, None),
            P(AXES, None),
            P(None, AXES),
            P(AXES),
            P(AXES),
            P(AXES),
            P(AXES),
            P(AXES),
        ),
        out_specs=(
            P("dp", "seq", None),
            P("dp", "seq", None),
            P("dp", "seq", None),
            P(AXES, None),
            P(AXES, None),
            P(AXES, None),
            P(AXES, None),
            P(AXES, None),
            P(AXES, None),
            P(AXES, None),
            P(None, AXES),
            P(AXES),
            P(AXES),
            P(AXES),
            P(AXES),
            P(AXES),
        ),
        check_vma=False,
    )
```

```python
from functools import partial

import jax
import jax.numpy as jnp
import numpy as np
from jax import lax
from jax.experimental import pallas as pl
from jax.experimental.pallas import tpu as pltpu
from jax.sharding import PartitionSpec as P

HEADS = 8
HEAD = 128
BUCKETS = 32
MAX_DIST = 128
EPS = 1e-05
NEG = -1e30
SCALE = HEAD ** (-0.5)
AXES = ("dp", "seq")
F32 = jnp.float32
BF16 = jnp.bfloat16
MIB = 1 << 20
VMEM_LIMIT = 60 * MIB
LOG2E = 1.4426950408889634
NO_COST = pl.CostEstimate(flops=0, bytes_accessed=0, transcendentals=0)
Q_SCALE = SCALE * LOG2E


def bucket_of(length):
    dist = np.arange(length)
    exact = BUCKETS // 2
    scaled = np.log(np.maximum(dist, exact) / exact) / np.log(MAX_DIST / exact) * (BUCKETS - exact)
    far = np.minimum(exact + np.floor(scaled).astype(np.int32), BUCKETS - 1)
    return np.where(dist < exact, dist, far).astype(np.int32)


def dot_nn(a, b):
    return jnp.dot(a, b, preferred_element_type=F32)


def dot_nt(a, b):
    return lax.dot_general(a, b, (((1,), (1,)), ((), ())), preferred_element_type=F32)


def norm_parts(x):
    mean = jnp.mean(x, axis=-1, keepdims=True)
    centered = x - mean
    spread = jnp.mean(centered * centered, axis=-1, keepdims=True)
    rstd = lax.rsqrt(spread + EPS)
    return centered * rstd, rstd


def norm_back(x, gain, dy):
    xhat, rstd = norm_parts(x)
    dyg = dy * gain
    mean_one = jnp.mean(dyg, axis=-1, keepdims=True)
    mean_two = jnp.mean(dyg * xhat, axis=-1, keepdims=True)
    return rstd * (dyg - mean_one - xhat * mean_two), dy * xhat


def row_iota(rows, cols):
    return lax.broadcasted_iota(jnp.int32, (rows, cols), 0)


def columns(start, size):
    return slice(start, start + size)


def pipeline(count, first, second, third):
    one, two = {}, {}
    for i in range(count + 2):
        if i < count:
            one[i] = first(i)
        if i >= 2:
            third(i - 2, two.pop(i - 2))
        if 1 <= i <= count:
            two[i - 1] = second(i - 1, one.pop(i - 1))


def start_all(pairs, sem, base=0):
    copies = [pltpu.make_async_copy(src, dst, sem.at[base + n]) for n, (src, dst) in enumerate(pairs)]
    for copy in copies:
        copy.start()
    return copies


def wait_all(copies):
    for copy in copies:
        copy.wait()


def soft_forward(one, two):
    top = jnp.maximum(jnp.max(one, axis=0, keepdims=True), jnp.max(two, axis=0, keepdims=True))
    one = jnp.exp2(one - top)
    two = jnp.exp2(two - top)
    total = jnp.sum(one, axis=0, keepdims=True) + jnp.sum(two, axis=0, keepdims=True)
    return one.astype(BF16), two.astype(BF16), 1.0 / total, top + jnp.log2(total)


def soft_backward(one, two, done, dtwo, lse):
    one = jnp.exp2(one - lse)
    two = jnp.exp2(two - lse)
    inner = jnp.sum(one * done, axis=0, keepdims=True) + jnp.sum(two * dtwo, axis=0, keepdims=True)
    return one.astype(BF16), two.astype(BF16), one * (done - inner), two * (dtwo - inner)


def row_chunks(rows, chunk, body):
    def step(i, carry):
        body(pl.ds(pl.multiple_of(i * chunk, chunk), chunk))
        return carry

    lax.fori_loop(0, rows // chunk, step, 0)


HBM = pl.BlockSpec(memory_space=pltpu.HBM)
SMEM = pl.BlockSpec(memory_space=pltpu.SMEM)
VMEM = pl.BlockSpec(memory_space=pltpu.VMEM)
CHUNK = 128
A_KV, A_STATE, A_MERGE, A_INIT, A_VEC, A_END = 0, 2048, 5120, 6144, 6656, 6784
B_Q, B_OUT, B_UP, B_DOWN, B_END = 0, 1024, 2048, 6144, 10240


def shape(dims, kind):
    return jax.ShapeDtypeStruct(dims, kind)


def advance_kernel(first, flags_ref, gains_ref, c_hbm, wa_hbm, kv_hbm, *refs):
    if first:
        x_hbm = c_hbm
        (kv_out, h1_out) = refs[:2]
        refs = refs[2:]
    else:
        refs = refs[6:]
    (new_hbm, cs_hbm, hc_hbm, ckvq_hbm, upd_hbm, z_hbm, lse_hbm) = refs[:7]
    refs = refs[7:]
    (c_v, w_v, m_v, kv_v, hc_v, ckvq_v, upd_v, z_v, new_v, lse_v, sem) = refs[:11]
    states, width = c_v.shape
    w_src = wa_hbm.at[:, pl.ds(A_STATE, 3 * width)]
    m_src = wa_hbm.at[:, pl.ds(A_MERGE, width)]
    if first:
        x_v, wkv_v, h1_v, init_v = refs[11:]
        begun = start_all(
            (
                (x_hbm, x_v),
                (wa_hbm.at[:, pl.ds(A_KV, 2 * width)], wkv_v),
                (wa_hbm.at[:, pl.ds(A_INIT, states)], init_v),
                (w_src, w_v),
                (m_src, m_v),
            ),
            sem,
            8,
        )
        begun[0].wait()

        def token_chunk(rows):
            xhat, _ = norm_parts(x_v[rows, :].astype(F32))
            h1_v[rows, :] = (xhat * gains_ref[0:1, :]).astype(BF16)

        row_chunks(x_v.shape[0], CHUNK, token_chunk)
        begun[1].wait()
        for t in range(4):
            cols = columns(512 * t, 512)
            kv_v[:, cols] = dot_nn(h1_v[...], wkv_v[:, cols]).astype(BF16)
        sent = start_all(((kv_v, kv_out), (h1_v, h1_out)), sem, 13)
        wait_all(begun[2:])

    @pl.when(flags_ref[0] == 1)
    def _():
        if first:
            c_v[...] = init_v[...].T
            begun_here = []
        else:
            begun_here = start_all(
                ((c_hbm, c_v), (w_src, w_v), (kv_hbm, kv_v), (m_src, m_v)), sem, 8
            )
            begun_here[0].wait()
        outs = start_all(((c_v, cs_hbm),), sem)

        def norm_chunk(rows):
            xhat, _ = norm_parts(c_v[rows, :].astype(F32))
            hc_v[rows, :] = (xhat * gains_ref[2:3, :]).astype(BF16)

        row_chunks(states, CHUNK, norm_chunk)
        outs += start_all(((hc_v, hc_hbm),), sem, 1)
        for copy in begun_here[1:2]:
            copy.wait()
        for t in range(6):
            cols = columns(512 * t, 512)
            product = dot_nn(hc_v[...], w_v[:, cols])
            ckvq_v[:, cols] = (product if t < 4 else product * Q_SCALE).astype(BF16)
        outs += start_all(((ckvq_v, ckvq_hbm),), sem, 2)
        wait_all(begun_here[2:])
        nvalid = flags_ref[1]
        allowed = row_iota(kv_v.shape[0], states) < nvalid

        def scores(h):
            q = ckvq_v[:, columns(2 * width + h * HEAD, HEAD)]
            return (
                dot_nt(ckvq_v[:, columns(h * HEAD, HEAD)], q),
                dot_nt(kv_v[:, columns(h * HEAD, HEAD)], q),
            )

        def soft(h, pair):
            return soft_forward(pair[0], jnp.where(allowed, pair[1], NEG))

        def mix(h, parts):
            one, two, factor, lse = parts
            mixed = dot_nn(ckvq_v[:, columns(width + h * HEAD, HEAD)].T, one)
            mixed += dot_nn(kv_v[:, columns(width + h * HEAD, HEAD)].T, two)
            upd_v[:, columns(h * HEAD, HEAD)] = (mixed * factor).T.astype(BF16)
            lse_v[h : h + 1, :] = lse

        pipeline(HEADS, scores, soft, mix)
        outs += start_all(((upd_v, upd_hbm), (lse_v, lse_hbm)), sem, 3)
        z_v[...] = dot_nn(upd_v[...], m_v[...])
        outs += start_all(((z_v, z_hbm),), sem, 5)

        def gate_chunk(rows):
            gate = gains_ref[3:4, :]
            new = gate * c_v[rows, :].astype(F32) + (1.0 - gate) * z_v[rows, :]
            new_v[rows, :] = new.astype(BF16)

        row_chunks(states, CHUNK, gate_chunk)
        outs += start_all(((new_v, new_hbm),), sem, 6)
        wait_all(outs)

    if first:
        wait_all(sent)


def advance(flags, gains, c, wa, kv, stash):
    states, width = c.shape
    rows = states if kv is None else kv.shape[0]
    first = stash is None
    extra = () if first else tuple(stash)
    shapes = [
        shape((states, width), BF16),
        shape((states, width), BF16),
        shape((states, width), BF16),
        shape((states, 3 * width), BF16),
        shape((states, width), BF16),
        shape((states, width), F32),
        shape((HEADS, states), F32),
    ]
    scratch = [
        pltpu.VMEM((states, width), BF16),
        pltpu.VMEM((width, 3 * width), BF16),
        pltpu.VMEM((width, width), BF16),
        pltpu.VMEM((rows, 2 * width), BF16),
        pltpu.VMEM((states, width), BF16),
        pltpu.VMEM((states, 3 * width), BF16),
        pltpu.VMEM((states, width), BF16),
        pltpu.VMEM((states, width), F32),
        pltpu.VMEM((states, width), BF16),
        pltpu.VMEM((HEADS, states), F32),
        pltpu.SemaphoreType.DMA((15,)),
    ]
    if first:
        kernel = lambda f, g, x, w, *refs: advance_kernel(True, f, g, x, w, None, *refs)
        shapes = [shape((rows, 2 * width), BF16), shape((rows, width), BF16)] + shapes
        scratch += [
            pltpu.VMEM((rows, width), BF16),
            pltpu.VMEM((width, 2 * width), BF16),
            pltpu.VMEM((rows, width), BF16),
            pltpu.VMEM((width, states), BF16),
        ]
        args = (flags, gains, c, wa)
    else:
        kernel = partial(advance_kernel, False)
        args = (flags, gains, c, wa, kv) + extra
    return pl.pallas_call(
        kernel,
        in_specs=[SMEM, VMEM] + [HBM] * (len(args) - 2),
        out_specs=[HBM] * len(shapes),
        out_shape=shapes,
        scratch_shapes=scratch,
        input_output_aliases={} if first else {5 + i: 1 + i for i in range(6)},
        compiler_params=pltpu.CompilerParams(vmem_limit_bytes=VMEM_LIMIT),
        cost_estimate=pl.CostEstimate(flops=9 << 30, bytes_accessed=24 * MIB, transcendentals=4 * MIB),
        name="advance",
    )(*args)


def bias_tiles(t_row):
    spread = jnp.broadcast_to(t_row, (128, t_row.shape[1]))
    grid = pltpu.roll(spread, 0, axis=1, stride=1, stride_axis=0)
    lane = lax.broadcasted_iota(jnp.int32, (128, 128), 1)
    sub = lax.broadcasted_iota(jnp.int32, (128, 128), 0)
    tiles = [grid[:, 128 * d : 128 * d + 128] for d in range(4)]
    tiles[0] = jnp.where(lane >= sub, tiles[0], NEG)
    return tiles


def bias_part(tiles, part):
    none = jnp.full((128, 128), NEG, F32)
    rows = []
    for j in range(2 * part + 2):
        row = [tiles[i - j] if i >= j else none for i in (2 * part, 2 * part + 1)]
        rows.append(jnp.concatenate(row, axis=1))
    return jnp.concatenate(rows, axis=0)


def block_kernel(flags_ref, t_ref, gains_ref, x_hbm, g_hbm, h1_hbm, kv_hbm, ckvq_hbm, wb_hbm,
                 o_hbm, x1_hbm, h2_hbm, act_hbm, dup_hbm, dx1_hbm, da_hbm, dq_hbm, dkv_hbm, dst_hbm,
                 db_ref, sums_ref,
                 x_v, g_v, q_v, kv_v, ckv_v, wo_v, wu_v, wd_v, o_v, x1_v, h2_v, act_v, dup_v,
                 dh_v, do_v, dq_v, dkv_v, dst_v, lse_v, wq_v, sem):
    rows, width = x_v.shape
    half = HEADS // 2 * HEAD
    loads = []
    for s in range(2):
        here, there = pl.ds(s * half, half), pl.ds(width + s * half, half)
        loads += [
            (wb_hbm.at[:, pl.ds(B_Q + s * half, half)], wq_v.at[:, here]),
            (ckvq_hbm.at[:, here], ckv_v.at[:, here]),
            (kv_hbm.at[:, here], kv_v.at[:, here]),
            (ckvq_hbm.at[:, there], ckv_v.at[:, there]),
            (kv_hbm.at[:, there], kv_v.at[:, there]),
        ]
    loads += [
        (wb_hbm.at[:, pl.ds(B_OUT, width)], wo_v),
        (x_hbm, x_v),
        (g_hbm, g_v),
        (wb_hbm.at[:, pl.ds(B_UP, 4 * width)], wu_v),
        (wb_hbm.at[:, pl.ds(B_DOWN, 4 * width)], wd_v),
    ]
    h1_in = start_all([(h1_hbm, do_v)], sem, 26)
    begun = start_all(loads, sem)
    wait_all(h1_in)
    nvalid = flags_ref[1]
    units = [(h, part) for h in range(HEADS) for part in range(2)]
    tile_cache = {}

    def tiles_of(h, key):
        if (h, key) not in tile_cache:
            tile_cache.clear()
            tile_cache[(h, key)] = bias_tiles(t_ref[h : h + 1, :])
        return tile_cache[(h, key)]

    def pick(n):
        h, part = units[n]
        return h, part, columns(256 * part, 256), 256 * (part + 1), columns(h * HEAD, HEAD), columns(width + h * HEAD, HEAD)

    def masked(scores, h, part, key):
        scores = scores + bias_part(tiles_of(h, key), part)
        return jnp.where(row_iota(scores.shape[0], 256) < nvalid, scores, NEG)

    def scores(n):
        h, part, span, used, here, there = pick(n)
        if part == 0 and h in (0, HEADS // 2):
            s = h // (HEADS // 2)
            wait_all(begun[5 * s :][:5])
            cols = columns(s * half, half)
            q_v[:, cols] = (dot_nn(do_v[...], wq_v[:, cols]) * Q_SCALE).astype(BF16)
        q = q_v[span, here]
        return dot_nt(ckv_v[:, here], q), dot_nt(kv_v[:used, here], q)

    def soft(n, pair):
        h, part, span, used, here, there = pick(n)
        return soft_forward(pair[0], masked(pair[1], h, part, 0))

    def mix(n, parts):
        h, part, span, used, here, there = pick(n)
        one, two, factor, lse = parts
        mixed = dot_nn(ckv_v[:, there].T, one) + dot_nn(kv_v[:used, there].T, two)
        o_v[span, here] = (mixed * factor).T.astype(BF16)
        lse_v[h : h + 1, span] = lse

    pipeline(len(units), scores, soft, mix)
    wait_all(begun[10:12])
    x1_v[...] = x_v[...].astype(F32) + dot_nn(o_v[...], wo_v[...])

    def norm_chunk(span):
        xhat, _ = norm_parts(x1_v[span, :])
        h2_v[span, :] = (xhat * gains_ref[1:2, :]).astype(BF16)

    row_chunks(rows, CHUNK, norm_chunk)
    outs = start_all(((o_v, o_hbm), (x1_v, x1_hbm), (h2_v, h2_hbm)), sem, 16)
    wait_all(begun[12:15])

    tile = 512

    def hidden(i):
        slab = wd_v[columns(tile * (i % 2), tile), columns(width * (i // 2), width)]
        return dot_nn(h2_v[...], wu_v[:, columns(tile * i, tile)]), dot_nt(g_v[...], slab)

    def activate(i, pair):
        up, dact = pair
        root = 0.7978845608028654
        square = up * up
        th = jnp.tanh(up * (root + (root * 0.044715) * square))
        part = 0.5 + 0.5 * th
        slope = part + up * (part - part * part) * (2 * root + (6 * root * 0.044715) * square)
        act_v[:, columns(tile * i, tile)] = (up * part).astype(BF16)
        dup_v[:, columns(tile * i, tile)] = (dact * slope).astype(BF16)

    pipeline(4 * width // tile, hidden, activate, lambda i, nothing: None)
    outs += start_all(((act_v, act_hbm), (dup_v, dup_hbm)), sem, 19)
    dh_v[...] = dot_nt(dup_v[...], wu_v[...])
    sums_ref[...] = jnp.zeros_like(sums_ref)

    def back_chunk(span):
        dx, gain_term = norm_back(x1_v[span, :], gains_ref[1:2, :], dh_v[span, :])
        dx = dx + g_v[span, :].astype(F32)
        dh_v[span, :] = dx
        x_v[span, :] = dx.astype(BF16)
        sums_ref[0:1, :] += jnp.sum(gain_term, axis=0, keepdims=True)

    row_chunks(rows, CHUNK, back_chunk)
    outs += start_all(((dh_v, dx1_hbm), (x_v, da_hbm)), sem, 21)
    do_v[...] = dot_nt(x_v[...], wo_v[...]).astype(BF16)

    held = {}

    def back_scores(n):
        h, part, span, used, here, there = pick(n)
        q, do = q_v[span, here], do_v[span, here]
        return (
            dot_nt(ckv_v[:, here], q),
            dot_nt(kv_v[:used, here], q),
            dot_nt(ckv_v[:, there], do),
            dot_nt(kv_v[:used, there], do),
        )

    def back_soft(n, parts):
        h, part, span, used, here, there = pick(n)
        lse = lse_v[h : h + 1, span]
        p1, p2, d1, d2 = soft_backward(
            parts[0], masked(parts[1], h, part, 1), parts[2], parts[3], lse
        )
        shear = held.setdefault(("shear", h), [0.0] * 4)
        for j in range(2 * part + 2):
            for i in (0, 1):
                d = 2 * part + i - j
                if d >= 0:
                    shear[d] = shear[d] + d2[128 * j : 128 * j + 128, 128 * i : 128 * i + 128]
        if part == 1:
            grid = jnp.concatenate(held.pop(("shear", h)), axis=1)
            size = grid.shape[1]
            flipped = grid[:8]
            for group in range(1, 16):
                flipped += pltpu.roll(grid[8 * group : 8 * group + 8], size - 8 * group, axis=1)
            for step in (1, 2, 4):
                moved = pltpu.roll(flipped, size - step, axis=1)
                flipped = jnp.where((row_iota(8, size) // step) % 2 == 1, moved, flipped)
            db_ref[h : h + 1, :] = jnp.sum(flipped, axis=0, keepdims=True)
        return p1, p2, d1.astype(BF16), d2.astype(BF16)

    def back_mix(n, parts):
        h, part, span, used, here, there = pick(n)
        p1, p2, d1, d2 = parts
        q, do = q_v[span, here], do_v[span, here]
        terms = [dot_nn(d1, q), dot_nn(p1, do), dot_nn(d2, q), dot_nn(p2, do)]
        dqt = dot_nn(ckv_v[:, here].T, d1) + dot_nn(kv_v[:used, here].T, d2)
        dq_v[span, here] = (dqt.T * SCALE).astype(BF16)
        if part == 0:
            held[("terms", h)] = terms
            return
        before = held.pop(("terms", h))
        dst_v[:, here] = ((before[0] + terms[0]) * (1.0 / LOG2E)).astype(BF16)
        dst_v[:, there] = (before[1] + terms[1]).astype(BF16)
        dkv_v[:256, here] = ((before[2] + terms[2][:256]) * (1.0 / LOG2E)).astype(BF16)
        dkv_v[256:, here] = (terms[2][256:] * (1.0 / LOG2E)).astype(BF16)
        dkv_v[:256, there] = (before[3] + terms[3][:256]).astype(BF16)
        dkv_v[256:, there] = terms[3][256:].astype(BF16)

    pipeline(len(units), back_scores, back_soft, back_mix)
    outs += start_all(((dq_v, dq_hbm), (dkv_v, dkv_hbm), (dst_v, dst_hbm)), sem, 23)
    wait_all(outs)


def block_part(flags, t, gains, x, g, h1, kv, ckvq, wb):
    rows, width = x.shape
    states = ckvq.shape[0]
    hidden = 4 * width
    narrow, wide = shape((rows, width), BF16), shape((rows, width), F32)
    return pl.pallas_call(
        block_kernel,
        in_specs=[SMEM, VMEM, VMEM] + [HBM] * 6,
        out_specs=[HBM] * 10 + [VMEM] * 2,
        out_shape=[
            narrow,
            wide,
            narrow,
            shape((rows, hidden), BF16),
            shape((rows, hidden), BF16),
            wide,
            narrow,
            narrow,
            shape((rows, 2 * width), BF16),
            shape((states, 2 * width), BF16),
            shape((HEADS, rows), F32),
            shape((8, width), F32),
        ],
        scratch_shapes=[
            pltpu.VMEM((rows, width), BF16),
            pltpu.VMEM((rows, width), BF16),
            pltpu.VMEM((rows, width), BF16),
            pltpu.VMEM((rows, 2 * width), BF16),
            pltpu.VMEM((states, 2 * width), BF16),
            pltpu.VMEM((width, width), BF16),
            pltpu.VMEM((width, hidden), BF16),
            pltpu.VMEM((width, hidden), BF16),
            pltpu.VMEM((rows, width), BF16),
            pltpu.VMEM((rows, width), F32),
            pltpu.VMEM((rows, width), BF16),
            pltpu.VMEM((rows, hidden), BF16),
            pltpu.VMEM((rows, hidden), BF16),
            pltpu.VMEM((rows, width), F32),
            pltpu.VMEM((rows, width), BF16),
            pltpu.VMEM((rows, width), BF16),
            pltpu.VMEM((rows, 2 * width), BF16),
            pltpu.VMEM((states, 2 * width), BF16),
            pltpu.VMEM((HEADS, rows), F32),
            pltpu.VMEM((width, width), BF16),
            pltpu.SemaphoreType.DMA((27,)),
        ],
        compiler_params=pltpu.CompilerParams(vmem_limit_bytes=VMEM_LIMIT),
        cost_estimate=pl.CostEstimate(flops=25 << 30, bytes_accessed=40 * MIB, transcendentals=10 * MIB),
        name="block_part",
    )(flags, t, gains, x, g, h1, kv, ckvq, wb)


def retreat_kernel(first, looped, flags_ref, gains_ref, lam_hbm, wa_hbm, kv_hbm, cs_hbm, ckvq_hbm, z_hbm,
                   lse_hbm, dst_hbm, *refs):
    if not first:
        refs = refs[4:]
    (prev_hbm, dz_hbm, dcs_hbm, dkv_hbm, sums_hbm) = refs[:5]
    (lam_v, w_v, m_v, kv_v, c_v, ckvq_v, z_v, lse_v, dst_v,
     dz_v, du_v, dcs_v, dkv_v, dh_v, prev_v, sums_v, sem) = refs[5:]
    states, width = c_v.shape

    @pl.when(flags_ref[0] == 1)
    def _():
        begun = start_all(
            (
                (lam_hbm, lam_v),
                (cs_hbm, c_v),
                (z_hbm, z_v),
                (wa_hbm.at[:, pl.ds(A_MERGE, width)], m_v),
                (ckvq_hbm, ckvq_v),
                (kv_hbm, kv_v),
                (lse_hbm, lse_v),
                (dst_hbm, dst_v),
                (wa_hbm.at[:, pl.ds(A_STATE, 3 * width)], w_v),
            ),
            sem,
        )
        wait_all(begun[:3])
        sums_v[...] = jnp.zeros_like(sums_v)

        def gate_chunk(rows):
            lam = lam_v[rows, :].astype(F32)
            dz_v[rows, :] = ((1.0 - gains_ref[3:4, :]) * lam).astype(BF16)
            change = lam * (c_v[rows, :].astype(F32) - z_v[rows, :])
            sums_v[1:2, :] += jnp.sum(change, axis=0, keepdims=True)

        row_chunks(states, CHUNK, gate_chunk)
        outs = start_all(((dz_v, dz_hbm),), sem, 9)
        begun[3].wait()
        du_v[...] = dot_nt(dz_v[...], m_v[...]).astype(BF16)
        wait_all(begun[4:8])
        allowed = row_iota(kv_v.shape[0], states) < flags_ref[1]

        def pick(h):
            starts = [base + h * HEAD for base in (0, width, 2 * width)]
            return [pl.ds(pl.multiple_of(n, HEAD) if looped else n, HEAD) for n in starts]

        def scores(h):
            here, there, third = pick(h)
            q, du = ckvq_v[:, third], du_v[:, here]
            return (
                dot_nt(ckvq_v[:, here], q),
                dot_nt(kv_v[:, here], q),
                dot_nt(ckvq_v[:, there], du),
                dot_nt(kv_v[:, there], du),
            )

        def soft(h, parts):
            one, two, done, dtwo = parts
            two = jnp.where(allowed, two, NEG)
            p1, p2, d1, d2 = soft_backward(one, two, done, dtwo, lse_v[pl.ds(h, 1), :])
            return p1, p2, d1.astype(BF16), d2.astype(BF16)

        def mix(h, parts):
            here, there, third = pick(h)
            p1, p2, d1, d2 = parts
            q, du = ckvq_v[:, third], du_v[:, here]
            ln2 = 1.0 / LOG2E
            dcs_v[:, here] = (dot_nn(d1, q) * ln2 + dst_v[:, here].astype(F32)).astype(BF16)
            dcs_v[:, there] = (dot_nn(p1, du) + dst_v[:, there].astype(F32)).astype(BF16)
            dkv_v[:, here] = (dot_nn(d2, q) * ln2).astype(BF16)
            dkv_v[:, there] = dot_nn(p2, du).astype(BF16)
            dqt = dot_nn(ckvq_v[:, here].T, d1) + dot_nn(kv_v[:, here].T, d2)
            dcs_v[:, third] = (dqt.T * SCALE).astype(BF16)

        def some(block, carry):
            base = 2 * block
            pipeline(2, lambda h: scores(base + h), lambda h, p: soft(base + h, p), lambda h, p: mix(base + h, p))
            return carry

        if looped:
            lax.fori_loop(0, HEADS // 2, some, 0)
        else:
            pipeline(HEADS, scores, soft, mix)
        outs += start_all(((dcs_v, dcs_hbm), (dkv_v, dkv_hbm)), sem, 10)
        begun[8].wait()
        dh_v[...] = dot_nt(dcs_v[...], w_v[...])

        def norm_chunk(rows):
            dx, gain_term = norm_back(c_v[rows, :].astype(F32), gains_ref[2:3, :], dh_v[rows, :])
            prev = dx + gains_ref[3:4, :] * lam_v[rows, :].astype(F32)
            prev_v[rows, :] = prev.astype(BF16)
            sums_v[0:1, :] += jnp.sum(gain_term, axis=0, keepdims=True)

        row_chunks(states, CHUNK, norm_chunk)
        outs += start_all(((prev_v, prev_hbm), (sums_v, sums_hbm)), sem, 12)
        wait_all(outs)


def retreat(flags, gains, lam, wa, kv, cs, ckvq, z, lse, dst, stash, looped):
    states, width = cs.shape
    rows = kv.shape[0]
    first = stash is None
    extra = () if first else tuple(stash)
    out = pl.pallas_call(
        partial(retreat_kernel, first, looped),
        in_specs=[SMEM, VMEM] + [HBM] * (8 + len(extra)),
        out_specs=[HBM] * 5,
        out_shape=[
            shape((states, width), BF16),
            shape((states, width), BF16),
            shape((states, 3 * width), BF16),
            shape((rows, 2 * width), BF16),
            shape((8, width), F32),
        ],
        scratch_shapes=[
            pltpu.VMEM((states, width), lam.dtype),
            pltpu.VMEM((width, 3 * width), BF16),
            pltpu.VMEM((width, width), BF16),
            pltpu.VMEM((rows, 2 * width), BF16),
            pltpu.VMEM((states, width), BF16),
            pltpu.VMEM((states, 3 * width), BF16),
            pltpu.VMEM((states, width), F32),
            pltpu.VMEM((HEADS, states), F32),
            pltpu.VMEM((states, 2 * width), BF16),
            pltpu.VMEM((states, width), BF16),
            pltpu.VMEM((states, width), BF16),
            pltpu.VMEM((states, 3 * width), BF16),
            pltpu.VMEM((rows, 2 * width), BF16),
            pltpu.VMEM((states, width), F32),
            pltpu.VMEM((states, width), BF16),
            pltpu.VMEM((8, width), F32),
            pltpu.SemaphoreType.DMA((14,)),
        ],
        input_output_aliases={} if first else {10 + i: 1 + i for i in range(4)},
        compiler_params=pltpu.CompilerParams(vmem_limit_bytes=VMEM_LIMIT),
        cost_estimate=pl.CostEstimate(flops=13 << 30, bytes_accessed=32 * MIB, transcendentals=4 * MIB),
        name="retreat",
    )(flags, gains, lam, wa, kv, cs, ckvq, z, lse, dst, *extra)
    return out[0], list(out[1:])


def input_grad_kernel(gains_ref, x_hbm, dx1_hbm, dq_hbm, one_hbm, two_hbm, wa_hbm, wb_hbm, out_hbm, sums_ref,
                      x_v, dx_v, dq_v, one_v, two_v, wkv_v, wq_v, dh_v, sem):
    rows, width = x_v.shape
    begun = start_all(
        (
            (one_hbm, one_v),
            (two_hbm, two_v),
            (wa_hbm.at[:, pl.ds(A_KV, 2 * width)], wkv_v),
            (dq_hbm, dq_v),
            (wb_hbm.at[:, pl.ds(B_Q, width)], wq_v),
            (x_hbm, x_v),
            (dx1_hbm, dx_v),
        ),
        sem,
    )
    wait_all(begun[:2])
    one_v[...] = (one_v[...].astype(F32) + two_v[...].astype(F32)).astype(BF16)
    begun[2].wait()
    dh_v[...] = dot_nt(one_v[...], wkv_v[...])
    wait_all(begun[3:5])
    dh_v[...] += dot_nt(dq_v[...], wq_v[...])
    wait_all(begun[5:])
    sums_ref[...] = jnp.zeros_like(sums_ref)

    def chunk(span):
        dx, gain_term = norm_back(x_v[span, :].astype(F32), gains_ref[0:1, :], dh_v[span, :])
        dx_v[span, :] += dx
        sums_ref[0:1, :] += jnp.sum(gain_term, axis=0, keepdims=True)

    row_chunks(rows, CHUNK, chunk)
    pltpu.sync_copy(dx_v, out_hbm)


def input_grad(gains, x, dx1, dq, one, two, wa, wb):
    rows, width = x.shape
    return pl.pallas_call(
        input_grad_kernel,
        in_specs=[VMEM] + [HBM] * 7,
        out_specs=[HBM, VMEM],
        out_shape=[shape((rows, width), F32), shape((8, width), F32)],
        scratch_shapes=[
            pltpu.VMEM((rows, width), BF16),
            pltpu.VMEM((rows, width), F32),
            pltpu.VMEM((rows, width), BF16),
            pltpu.VMEM((rows, 2 * width), BF16),
            pltpu.VMEM((rows, 2 * width), BF16),
            pltpu.VMEM((width, 2 * width), BF16),
            pltpu.VMEM((width, width), BF16),
            pltpu.VMEM((rows, width), F32),
            pltpu.SemaphoreType.DMA((7,)),
        ],
        compiler_params=pltpu.CompilerParams(vmem_limit_bytes=VMEM_LIMIT),
        cost_estimate=NO_COST,
        name="input_grad",
    )(gains, x, dx1, dq, one, two, wa, wb)


def dot_tn(a, b):
    return lax.dot_general(a, b, (((0,), (0,)), ((), ())), preferred_element_type=F32)


def early_kernel(share, fresh, flags_ref, o_hbm, da_hbm, h1_hbm, dq_hbm, h2_hbm, dup_hbm, act_hbm, g_hbm, *refs):
    outs = refs[:-11] if fresh else refs[(len(refs) - 11) // 2 : -11]
    (o_v, da_v, h1_v, dq_v, h2_v, g_v, dup_v, act_v, tile_v, sem, out_sem) = refs[-11:]
    width = h2_v.shape[1]
    tile = tile_v.shape[-1]
    cut = B_END // 2
    mine = flags_ref[2]

    @pl.when(flags_ref[0] == 1)
    def _():
        begun = start_all(
            ((act_hbm, act_v), (g_hbm, g_v), (o_hbm, o_v), (da_hbm, da_v), (h1_hbm, h1_v), (dq_hbm, dq_v),
             (h2_hbm, h2_v), (dup_hbm, dup_v)), sem)

        def outgoing(slot, base, n):
            here = pl.multiple_of(base % cut + n * tile, tile)
            if share % 32:
                there = pl.ds(pl.multiple_of(base + n * tile, tile), tile)
                pairs = [(tile_v.at[slot], outs[0].at[:, there])]
            else:
                send, keep = outs[2 * (base // cut) : 2 * (base // cut) + 2]
                pairs = [
                    (tile_v.at[slot, :, 1 - mine], send.at[:, :, pl.ds(here, tile)]),
                    (tile_v.at[slot, :, mine], keep.at[:, :, pl.ds(here, tile)]),
                ]
            return [pltpu.make_async_copy(src, dst, out_sem.at[slot, m]) for m, (src, dst) in enumerate(pairs)]

        def emit(count, base, product, done):
            def step(n, carry):
                slot = n % 2
                copies = outgoing(slot, base, n)
                value = product(n).astype(BF16)

                @pl.when(n + done >= 2)
                def _():
                    wait_all(copies)

                tile_v[slot] = value.reshape(tile_v.shape[1:])
                for copy in copies:
                    copy.start()
                return carry

            lax.fori_loop(0, count, step, 0)

        def at(n):
            return pl.ds(pl.multiple_of(n * tile, tile), tile)

        def down(n):
            slab = pl.ds(pl.multiple_of((n // 2) * width, width), width)
            return dot_tn(act_v[:, slab], g_v[:, at(n % 2)])

        first = (cut - B_UP) // tile
        wait_all(begun[:2])
        emit(8, B_DOWN, down, 0)
        wait_all(begun[2:4])
        emit(2, B_OUT, lambda n: dot_tn(o_v[...], da_v[:, at(n)]), 8)
        wait_all(begun[4:6])
        emit(2, B_Q, lambda n: dot_tn(h1_v[...], dq_v[:, at(n)]), 10)
        wait_all(begun[6:8])
        emit(first, B_UP, lambda n: dot_tn(h2_v[...], dup_v[:, at(n)]), 12)
        emit(8 - first, cut, lambda n: dot_tn(h2_v[...], dup_v[:, at(n + first)]), 12 + first)
        for slot in range(2):
            wait_all(outgoing(slot, 0, 0))


def early_grads(flags, share, before, o, da, h1, dq, h2, dup, act, g):
    rows, width = o.shape
    pairs = width // (2 * share)
    if share % 32:
        outs = [shape((width, B_END), BF16)]
        tiles = pltpu.VMEM((2, width, 512), BF16)
    else:
        outs = [shape((pairs, share, B_END // 2), BF16)] * 4
        tiles = pltpu.VMEM((2, pairs, 2, share, 512), BF16)
    narrow = pltpu.VMEM((rows, width), BF16)
    wide = pltpu.VMEM((rows, 4 * width), BF16)
    return pl.pallas_call(
        partial(early_kernel, share, not before),
        in_specs=[SMEM] + [HBM] * (8 + len(before)),
        out_specs=[HBM] * len(outs),
        out_shape=outs,
        scratch_shapes=[narrow] * 6 + [wide] * 2 + [tiles, pltpu.SemaphoreType.DMA((8,)), pltpu.SemaphoreType.DMA((2, 2))],
        input_output_aliases={9 + n: n for n in range(len(before))},
        compiler_params=pltpu.CompilerParams(vmem_limit_bytes=VMEM_LIMIT),
        cost_estimate=pl.CostEstimate(flops=11 << 30, bytes_accessed=34 * MIB, transcendentals=0),
        name="early_grads",
    )(flags, o, da, h1, dq, h2, dup, act, g, *before)


def layer_out_kernel(x1_ref, act_ref, wd_ref, out_ref, acc_ref):
    i = pl.program_id(0)
    term = dot_nn(act_ref[...], wd_ref[...])

    @pl.when(i == 0)
    def _():
        acc_ref[...] = x1_ref[...] + term

    @pl.when(i > 0)
    def _():
        acc_ref[...] += term

    @pl.when(i == pl.num_programs(0) - 1)
    def _():
        out_ref[...] = acc_ref[...].astype(BF16)


def layer_output(x1, act, wb):
    rows, width = x1.shape
    return pl.pallas_call(
        layer_out_kernel,
        grid=(4,),
        in_specs=[
            pl.BlockSpec((rows, width), lambda i: (0, 0)),
            pl.BlockSpec((rows, width), lambda i: (0, i)),
            pl.BlockSpec((width, width), lambda i: (0, B_DOWN // width + i)),
        ],
        out_specs=pl.BlockSpec((rows, width), lambda i: (0, 0)),
        out_shape=shape((rows, width), BF16),
        scratch_shapes=[pltpu.VMEM((rows, width), F32)],
        compiler_params=pltpu.CompilerParams(vmem_limit_bytes=VMEM_LIMIT),
        cost_estimate=pl.CostEstimate(flops=4 << 30, bytes_accessed=15 * MIB, transcendentals=0),
        name="layer_output",
    )(x1, act, wb)


def late_kernel(plan, share, flags_ref, *refs):
    count = len(refs) - 2
    send_ref, keep_ref = refs[count:]
    mine = flags_ref[2] == 0
    tile = 512
    for n, (kind, a, b) in enumerate(plan):
        if kind == "product":
            value = dot_tn(refs[a][...], refs[b[0]][:, columns(b[1], tile)])
        elif kind == "sum":
            total = sum(refs[m][:, columns(b[1], tile)].astype(F32) for m in b[0])
            value = dot_tn(refs[a][...], total.astype(BF16))
        else:
            value = jnp.where(flags_ref[3] == 0, refs[a][...].T.astype(F32), 0.0)
        value = value.astype(BF16)
        cols = columns(n * tile, tile)
        for m in range(value.shape[0] // (2 * share)):
            low = value[2 * share * m : 2 * share * m + share]
            high = value[2 * share * m + share : 2 * share * (m + 1)]
            rows = columns(share * m, share)
            send_ref[rows, cols] = jnp.where(mine, high, low)
            keep_ref[rows, cols] = jnp.where(mine, low, high)


def late_whole_kernel(plan, flags_ref, *refs):
    tile = 512
    for n, (kind, a, b) in enumerate(plan):
        if kind == "product":
            value = dot_tn(refs[a][...], refs[b[0]][:, columns(b[1], tile)])
        elif kind == "sum":
            total = sum(refs[m][:, columns(b[1], tile)].astype(F32) for m in b[0])
            value = dot_tn(refs[a][...], total.astype(BF16))
        else:
            value = jnp.where(flags_ref[3] == 0, refs[a][...].T.astype(F32), 0.0)
        refs[-1][:, columns(n * tile, tile)] = value.astype(BF16)


def late_grads(flags, share, plan, *arrays):
    width = arrays[0].shape[1]
    cols = 512 * len(plan)
    params = dict(
        in_specs=[SMEM] + [VMEM] * len(arrays),
        compiler_params=pltpu.CompilerParams(vmem_limit_bytes=VMEM_LIMIT),
        cost_estimate=NO_COST,
        name="late_grads",
    )
    if share % 32:
        whole = pl.pallas_call(
            partial(late_whole_kernel, plan), out_specs=VMEM, out_shape=shape((width, cols), BF16), **params
        )(flags, *arrays)
        blocks = whole.reshape(width // (2 * share), 2, share, cols)
        keep = lax.dynamic_index_in_dim(blocks, flags[2], 1, keepdims=False)
        send = lax.dynamic_index_in_dim(blocks, 1 - flags[2], 1, keepdims=False)
        return send, keep
    half = shape((width // 2, cols), BF16)
    send, keep = pl.pallas_call(
        partial(late_kernel, plan, share), out_specs=[VMEM] * 2, out_shape=[half, half], **params
    )(flags, *arrays)
    dims = (width // (2 * share), share, cols)
    return send.reshape(dims), keep.reshape(dims)


def settle_kernel(devices, in_ref, q_ref, out_ref, up_ref, down_ref):
    share = in_ref.shape[0]
    width = share * devices
    q_ref[...] = in_ref[:, columns(B_Q, width)].astype(F32)
    out_ref[...] = in_ref[:, columns(B_OUT, width)].astype(F32)
    for d in range(devices):
        pieces = [in_ref[:, columns(B_UP + s * width + d * share, share)] for s in range(4)]
        up_ref[:, columns(4 * share * d, 4 * share)] = jnp.concatenate(pieces, axis=1).astype(F32)
    for s in range(4):
        down_ref[columns(s * share, share), :] = in_ref[:, columns(B_DOWN + s * width, width)].astype(F32)


def settle(early, devices):
    share = early.shape[0]
    width = share * devices
    return pl.pallas_call(
        partial(settle_kernel, devices),
        in_specs=[VMEM],
        out_specs=[VMEM] * 4,
        out_shape=[
            shape((share, width), F32),
            shape((share, width), F32),
            shape((share, 4 * width), F32),
            shape((4 * share, width), F32),
        ],
        compiler_params=pltpu.CompilerParams(vmem_limit_bytes=VMEM_LIMIT),
        name="settle",
    )(early)


def orders_of(devices):
    bits = [1 << n for n in range(devices.bit_length() - 1)]
    if devices != 32:
        return [bits] * 2, [bits] * 2
    core, x, y, z, far = bits
    return [[core, y, z, x, far], [core, z, y, x, far]], [[core, y, x, z, far], [core, z, y, x, far]]


def exchange(value, bit, devices):
    return lax.ppermute(value, AXES, [(i, i ^ bit) for i in range(devices)])


def split_blocks(term, place, which):
    blocks, rows, cols = term.shape
    low = 1 << place
    view = term.reshape(blocks // (2 * low), 2, low, rows, cols)
    return lax.dynamic_index_in_dim(view, which, 1, keepdims=False).reshape(blocks // 2, rows, cols)


def half_kernel(count, which_ref, *refs):
    pairs, outs = refs[: 2 * count], refs[2 * count : 3 * count]
    scratch, (sem, out_sem) = refs[3 * count : 5 * count], refs[5 * count :]
    loads, stores = [], []
    for n in range(count):
        which = which_ref[n]
        loads.append(
            start_all(
                [(pairs[2 * n + m].at[:, which], scratch[2 * n + m]) for m in range(2)], sem, 2 * n
            )
        )
    for n in range(count):
        wait_all(loads[n])
        one, two = scratch[2 * n], scratch[2 * n + 1]
        high, low = one.shape[:2]

        def add(i, carry, one=one, two=two, low=low):
            one[i // low, i % low] = (
                one[i // low, i % low].astype(F32) + two[i // low, i % low].astype(F32)
            ).astype(BF16)
            return carry

        lax.fori_loop(0, high * low, add, 0)
        stores += start_all([(one, outs[n])], out_sem, n)
    wait_all(stores)


def half_sums(terms, places, which):
    share = terms[0][0].shape[1]
    if share % 32:
        return [
            sum(split_blocks(t, place, w).astype(F32) for t in pair).astype(BF16)
            for pair, place, w in zip(terms, places, which)
        ]
    args, outs, scratch = [], [], []
    for pair, place in zip(terms, places):
        blocks, rows, cols = pair[0].shape
        low = 1 << place
        high = blocks // (2 * low)
        args += [t.reshape(high, 2, low, rows, cols) for t in pair]
        outs.append(shape((high, low, rows, cols), BF16))
        scratch += [pltpu.VMEM((high, low, rows, cols), BF16)] * 2
    count = len(terms)
    results = pl.pallas_call(
        partial(half_kernel, count),
        in_specs=[SMEM] + [HBM] * (2 * count),
        out_specs=[HBM] * count,
        out_shape=outs,
        scratch_shapes=scratch + [pltpu.SemaphoreType.DMA((2 * count,)), pltpu.SemaphoreType.DMA((count,))],
        compiler_params=pltpu.CompilerParams(vmem_limit_bytes=VMEM_LIMIT),
        cost_estimate=NO_COST,
        name="half_sums",
    )(jnp.stack(which), *args)
    return [r.reshape(-1, *r.shape[2:]) for r in results]


class Stream:
    def __init__(self, send, keep, order, devices):
        self.devices, self.order, self.left = devices, list(order), sorted(order)
        self.keep, self.send, self.got = keep, send, None
        self.bit = self.order.pop(0)
        self.left.remove(self.bit)

    def move(self):
        self.got = exchange(self.send, self.bit, self.devices)
        self.send = None

    def result(self):
        return (self.keep.astype(F32) + self.got.astype(F32))[0]


class Few:
    def __init__(self, value, order, devices):
        self.devices, self.order, self.left, self.total = devices, list(order), sorted(order), value.astype(F32)
        self.pick()

    def pick(self):
        me = lax.axis_index(AXES)
        bits, self.order = self.order[:2], self.order[2:]
        masks = [0]
        for bit in bits:
            masks += [mask | bit for mask in masks]
        parts = []
        for mask in masks:
            value, left = self.total, list(self.left)
            for bit in bits:
                value = split_blocks(value, left.index(bit), ((me ^ mask) // bit) % 2)
                left.remove(bit)
            parts.append(value)
        self.left = [bit for bit in self.left if bit not in bits]
        self.keep, self.send, self.masks = parts[0], [part.astype(BF16) for part in parts[1:]], masks[1:]

    def move(self):
        self.got = [exchange(send, mask, self.devices) for send, mask in zip(self.send, self.masks)]
        self.send = None

    def split(self):
        self.total = self.keep + sum(got.astype(F32) for got in self.got)
        self.pick()

    def result(self):
        return (self.keep + sum(got.astype(F32) for got in self.got))[0]


class Step:
    def __init__(self, streams):
        self.streams, self.terms, self.places, self.mine = streams, [], [], []
        for stream in streams:
            stream.bit = stream.order.pop(0)
            self.places.append(stream.left.index(stream.bit))
            stream.left.remove(stream.bit)
            self.mine.append((lax.axis_index(AXES) // stream.bit) % 2)
            self.terms.append((stream.keep, stream.got))
        sends = half_sums(self.terms, self.places, [1 - m for m in self.mine])
        for stream, send in zip(streams, sends):
            stream.send = send

    def keep(self, after):
        after, self.terms = lax.optimization_barrier((after, self.terms))
        keeps = half_sums(self.terms, self.places, self.mine)
        for stream, keep in zip(self.streams, keeps):
            stream.keep = keep
        return after


def split(streams):
    step = Step(streams)
    sends = step.keep([stream.send for stream in streams])
    for stream, send in zip(streams, sends):
        stream.send = send


def body(
    layer_input,
    segment_length,
    output_gradient,
    state_cotangent,
    query_key_value_weight,
    state_key_value_weight,
    state_query_weight,
    output_weight,
    merge_weight,
    up_weight,
    down_weight,
    initial_state_learned,
    attention_norm_gain,
    feedforward_norm_gain,
    state_norm_gain,
    state_gate_logits,
    relative_position_bias,
):
    _, rows, width = layer_input.shape
    place = lax.axis_index("seq")
    count = lax.axis_size("seq")
    devices = count * lax.axis_size("dp")
    share = width // devices
    pairs = lax.axis_size("dp")

    bias_local = relative_position_bias.shape[0]
    small = jnp.stack(
        [
            attention_norm_gain,
            feedforward_norm_gain,
            state_norm_gain,
            state_gate_logits,
            jnp.pad(relative_position_bias, (0, share - bias_local)),
        ],
        axis=1,
    )
    small = jnp.pad(small, ((0, 0), (0, A_END - A_VEC - 5)))
    wa = jnp.concatenate(
        [
            query_key_value_weight[:, width:],
            state_key_value_weight,
            state_query_weight,
            merge_weight,
            initial_state_learned.T,
            small,
        ],
        axis=1,
    )
    up_local = up_weight.reshape(share, devices, 4, share).transpose(0, 2, 1, 3)
    down_local = down_weight.reshape(4, share, width).transpose(1, 0, 2)
    wb = jnp.concatenate(
        [
            query_key_value_weight[:, :width],
            output_weight,
            up_local.reshape(share, 4 * width),
            down_local.reshape(share, 4 * width),
        ],
        axis=1,
    )
    wa = lax.all_gather(wa, AXES, axis=0, tiled=True)
    wb = lax.all_gather(wb, AXES, axis=0, tiled=True)

    vectors = wa[:, A_VEC : A_VEC + 5].astype(F32).T
    gate = jax.nn.sigmoid(vectors[3:4])
    gains = jnp.concatenate([vectors[:3], gate, jnp.zeros((4, width), F32)], axis=0)
    table = vectors[4].reshape(devices, share)[:, :bias_local].reshape(HEADS, BUCKETS)
    onehot = np.eye(BUCKETS, dtype=np.float32)[:, bucket_of(rows)]
    t = jnp.dot(table * LOG2E, jnp.asarray(onehot), precision=lax.Precision.HIGHEST)

    x = layer_input.reshape(rows, width)
    g = output_gradient.reshape(rows, width)
    nvalid = jnp.clip(segment_length[0] - place * rows, 0, rows).astype(jnp.int32)

    def flags(section):
        core = lax.axis_index(AXES) % 2
        parts = [(place == section).astype(jnp.int32), nvalid, core, place]
        return jnp.stack([part.astype(jnp.int32) for part in parts])

    def hop(value, frm, to):
        route = [(d * count + frm, d * count + to) for d in range(pairs)]
        return lax.ppermute(value, AXES, route)

    kv, h1, new, *stash = advance(flags(0), gains, x, wa, None, None)
    for section in range(1, count):
        carry = hop(new, section - 1, section)
        new, *stash = advance(flags(section), gains, carry, wa, kv, stash)
    cs, hc, ckvq, upd, z, lse_two = stash

    quarter = new.shape[0] // count
    state_out = lax.dynamic_slice_in_dim(new, place * quarter, quarter, 0)
    for to in range(count - 1):
        got = hop(new[to * quarter : (to + 1) * quarter], count - 1, to)
        state_out = jnp.where(place == to, got, state_out)
    wb, state_out = lax.optimization_barrier((wb, state_out))
    state_out = state_out.astype(F32)[None]

    o, x1, h2, act, dup, dx1, da, dq, dkv, dst, dbias, sums_mlp = block_part(
        flags(0), t, gains, x, g, h1, kv, ckvq, wb
    )

    early_args = (o, da, h1, dq, h2, dup, act, g)

    def only(active):
        parts = [active, nvalid, lax.axis_index(AXES) % 2]
        return jnp.stack([part.astype(jnp.int32) for part in parts])

    halves = early_grads(only(place < count - 1), share, (), *early_args)

    tie = lax.optimization_barrier
    early_orders, late_orders = orders_of(devices)
    back = None
    lam = state_cotangent.reshape(state_cotangent.shape[1:])
    lam, halves = tie((lam, halves))
    for section in reversed(range(count)):
        prev, back = retreat(flags(section), gains, lam, wa, kv, cs, ckvq, z, lse_two, dst, back, section > 0)
        if section == 0:
            break
        if section == count - 1:
            prev, halves = tie((prev, halves))
            lam = hop(prev, section, section - 1)
            halves = early_grads(only(place == count - 1), share, tuple(halves), *early_args)
            lam, halves = tie((lam, halves))
            if share % 32:
                whole = halves[0].reshape(devices, share, B_END)
                mine = lax.axis_index(AXES) % 2
                halves = [split_blocks(whole, 0, 1 - mine), split_blocks(whole, 0, mine)]
                cut = B_END // 2
                halves = [half[:, :, c : c + cut] for c in (0, cut) for half in halves]
        elif section == count - 2:
            prev, halves, x1 = tie((prev, halves, x1))
            early = [Stream(*halves[2 * n : 2 * n + 2], early_orders[n], devices) for n in range(2)]
            lam = hop(prev, section, section - 1)
            for stream in early:
                stream.move()
            layer_out = layer_output(x1, act, wb)
            layer_out, gots = tie((layer_out, [stream.got for stream in early]))
            for stream, got in zip(early, gots):
                stream.got = got
            step = Step(early)
            lam, sends = tie((lam, [stream.send for stream in early]))
            for stream, send in zip(early, sends):
                stream.send = send
                stream.move()
        else:
            prev = step.keep(prev)
            lam = hop(prev, section, section - 1)
            lam, keeps = tie((lam, [stream.keep for stream in early]))
            for stream, keep in zip(early, keeps):
                stream.keep = keep
    dz, dcs, dkv_two, sums_state = back

    tiles = [512 * n for n in range(4)]
    late_one = [("product", 0, (1, 512 * n)) for n in range(6)] + [("flip", 2, None)]
    late_two = [("sum", 0, ((1, 2), c)) for c in tiles] + [("product", 3, (4, c)) for c in tiles[:2]]
    def arrived(streams, others):
        gots, keeps, others = tie(([s.got for s in streams], [s.keep for s in streams], others))
        for stream, got, keep in zip(streams, gots, keeps):
            stream.got, stream.keep = got, keep
        return others

    def together(streams, other=None):
        sends = tie([stream.send for stream in streams])
        for stream, send in zip(streams, sends):
            stream.send = send
        result = other(jnp.minimum(jnp.abs(sends[0][0, 0, 0].astype(F32)), 0.0)) if other else ()
        for stream in streams:
            stream.move()
        return arrived(streams, result)

    prev, gots = tie((prev, [stream.got for stream in early]))
    for stream, got in zip(early, gots):
        stream.got = got
    split(early)
    switches = flags(0)
    switches, sends = tie((switches, [stream.send for stream in early]))
    for stream, send in zip(early, sends):
        stream.send = send
        stream.move()
    late = [
        late_grads(switches, share, late_one, hc, dcs, prev),
        late_grads(switches, share, late_two, h1, dkv, dkv_two, upd, dz),
    ]
    late = [Stream(*halves, order, devices) for halves, order in zip(arrived(early, late), late_orders)]
    for stream in late:
        stream.move()
    split(early)
    gots, sends, keeps = tie(
        ([s.got for s in late], [s.send for s in early], [s.keep for s in early])
    )
    for stream, got in zip(late, gots):
        stream.got = got
    for stream, send, keep in zip(early, sends, keeps):
        stream.send, stream.keep = send, keep
    split(late)
    x_grad, sums_attn = together(
        late + early, lambda zero: input_grad(gains + zero, x, dx1, dq, dkv, dkv_two, wa, wb)
    )

    buckets = jnp.asarray(np.ascontiguousarray(onehot.T))
    dtable = jnp.dot(dbias, buckets, precision=lax.Precision.HIGHEST).reshape(devices, bias_local)
    dtable = jnp.pad(dtable, ((0, 0), (0, share - bias_local))).reshape(width)
    gate_grad = sums_state[1] * gate[0] * (1.0 - gate[0])
    vectors = jnp.stack([sums_attn[0], sums_mlp[0], sums_state[0], gate_grad, dtable], axis=1)
    vectors = jnp.pad(vectors, ((0, 0), (0, 123))).reshape(devices, share, 128)
    small = Few(vectors, sorted(late_orders[0]), devices)
    while late[0].order or small.order or small.send:
        running = [stream for stream in late + early if stream.order]
        if running:
            split(running)
        if small.send is None and small.order:
            small.split()
        together(running + ([small] if small.send else []))
    early = jnp.concatenate([stream.result() for stream in early], axis=1)
    one, two = [stream.result() for stream in late]
    vec = small.result()

    q_shard, out_shard, up_shard, down_shard = settle(early, devices)
    return (
        layer_out[None],
        state_out,
        x_grad[None],
        jnp.concatenate([q_shard, two[:, : 2 * width]], axis=1),
        one[:, : 2 * width],
        one[:, 2 * width : 3 * width],
        out_shard,
        two[:, 2 * width :],
        up_shard,
        down_shard,
        one[:, 3 * width :].T,
        vec[:, 0],
        vec[:, 1],
        vec[:, 2],
        vec[:, 3],
        vec[:bias_local, 4],
    )


def solution(mesh):
    return jax.shard_map(
        body,
        mesh=mesh,
        in_specs=(
            P("dp", "seq", None),
            P("dp"),
            P("dp", "seq", None),
            P("dp", None, None),
            P(AXES, None),
            P(AXES, None),
            P(AXES, None),
            P(AXES, None),
            P(AXES, None),
            P(AXES, None),
            P(AXES, None),
            P(None, AXES),
            P(AXES),
            P(AXES),
            P(AXES),
            P(AXES),
            P(AXES),
        ),
        out_specs=(
            P("dp", "seq", None),
            P("dp", "seq", None),
            P("dp", "seq", None),
            P(AXES, None),
            P(AXES, None),
            P(AXES, None),
            P(AXES, None),
            P(AXES, None),
            P(AXES, None),
            P(AXES, None),
            P(None, AXES),
            P(AXES),
            P(AXES),
            P(AXES),
            P(AXES),
            P(AXES),
        ),
        check_vma=False,
    )
```

```python
from functools import partial

import jax
import jax.numpy as jnp
import numpy as np
from jax import lax
from jax.experimental import pallas as pl
from jax.experimental.pallas import tpu as pltpu
from jax.sharding import PartitionSpec as P

HEADS = 8
HEAD = 128
BUCKETS = 32
MAX_DIST = 128
EPS = 1e-05
NEG = -1e30
SCALE = HEAD ** (-0.5)
AXES = ("dp", "seq")
F32 = jnp.float32
BF16 = jnp.bfloat16
MIB = 1 << 20
VMEM_LIMIT = 60 * MIB
LOG2E = 1.4426950408889634
NO_COST = pl.CostEstimate(flops=0, bytes_accessed=0, transcendentals=0)
Q_SCALE = SCALE * LOG2E


def bucket_of(length):
    dist = np.arange(length)
    exact = BUCKETS // 2
    scaled = np.log(np.maximum(dist, exact) / exact) / np.log(MAX_DIST / exact) * (BUCKETS - exact)
    far = np.minimum(exact + np.floor(scaled).astype(np.int32), BUCKETS - 1)
    return np.where(dist < exact, dist, far).astype(np.int32)


def dot_nn(a, b):
    return jnp.dot(a, b, preferred_element_type=F32)


def dot_nt(a, b):
    return lax.dot_general(a, b, (((1,), (1,)), ((), ())), preferred_element_type=F32)


def norm_parts(x):
    mean = jnp.mean(x, axis=-1, keepdims=True)
    centered = x - mean
    spread = jnp.mean(centered * centered, axis=-1, keepdims=True)
    rstd = lax.rsqrt(spread + EPS)
    return centered * rstd, rstd


def norm_back(x, gain, dy):
    xhat, rstd = norm_parts(x)
    dyg = dy * gain
    mean_one = jnp.mean(dyg, axis=-1, keepdims=True)
    mean_two = jnp.mean(dyg * xhat, axis=-1, keepdims=True)
    return rstd * (dyg - mean_one - xhat * mean_two), dy * xhat


def row_iota(rows, cols):
    return lax.broadcasted_iota(jnp.int32, (rows, cols), 0)


def columns(start, size):
    return slice(start, start + size)


def pipeline(count, first, second, third):
    one, two = {}, {}
    for i in range(count + 2):
        if i < count:
            one[i] = first(i)
        if i >= 2:
            third(i - 2, two.pop(i - 2))
        if 1 <= i <= count:
            two[i - 1] = second(i - 1, one.pop(i - 1))


def start_all(pairs, sem, base=0):
    copies = [pltpu.make_async_copy(src, dst, sem.at[base + n]) for n, (src, dst) in enumerate(pairs)]
    for copy in copies:
        copy.start()
    return copies


def wait_all(copies):
    for copy in copies:
        copy.wait()


def soft_forward(one, two):
    top = jnp.maximum(jnp.max(one, axis=0, keepdims=True), jnp.max(two, axis=0, keepdims=True))
    one = jnp.exp2(one - top)
    two = jnp.exp2(two - top)
    total = jnp.sum(one, axis=0, keepdims=True) + jnp.sum(two, axis=0, keepdims=True)
    return one.astype(BF16), two.astype(BF16), 1.0 / total, top + jnp.log2(total)


def soft_backward(one, two, done, dtwo, lse):
    one = jnp.exp2(one - lse)
    two = jnp.exp2(two - lse)
    inner = jnp.sum(one * done, axis=0, keepdims=True) + jnp.sum(two * dtwo, axis=0, keepdims=True)
    return one.astype(BF16), two.astype(BF16), one * (done - inner), two * (dtwo - inner)


def row_chunks(rows, chunk, body):
    def step(i, carry):
        body(pl.ds(pl.multiple_of(i * chunk, chunk), chunk))
        return carry

    lax.fori_loop(0, rows // chunk, step, 0)


HBM = pl.BlockSpec(memory_space=pltpu.HBM)
SMEM = pl.BlockSpec(memory_space=pltpu.SMEM)
VMEM = pl.BlockSpec(memory_space=pltpu.VMEM)
CHUNK = 128
A_KV, A_STATE, A_MERGE, A_INIT, A_Q, A_VEC, A_END = 0, 2048, 5120, 6144, 6656, 7680, 7808
W_OUT, W_UP, W_DOWN = 0, 1024, 5120
B_Q, B_OUT, B_UP, B_DOWN, B_END = 0, 1024, 2048, 6144, 10240


def shape(dims, kind):
    return jax.ShapeDtypeStruct(dims, kind)


def advance_kernel(first, flags_ref, gains_ref, c_hbm, wa_hbm, kv_hbm, *refs):
    if first:
        x_hbm = c_hbm
        (kv_out, h1_out) = refs[:2]
        refs = refs[2:]
    else:
        refs = refs[6:]
    (new_hbm, cs_hbm, hc_hbm, ckvq_hbm, upd_hbm, z_hbm, lse_hbm) = refs[:7]
    refs = refs[7:]
    (c_v, w_v, m_v, kv_v, hc_v, ckvq_v, upd_v, z_v, new_v, lse_v, sem) = refs[:11]
    states, width = c_v.shape
    w_src = wa_hbm.at[:, pl.ds(A_STATE, 3 * width)]
    m_src = wa_hbm.at[:, pl.ds(A_MERGE, width)]
    if first:
        x_v, wkv_v, h1_v, init_v = refs[11:]
        begun = start_all(
            (
                (x_hbm, x_v),
                (wa_hbm.at[:, pl.ds(A_KV, 2 * width)], wkv_v),
                (wa_hbm.at[:, pl.ds(A_INIT, states)], init_v),
                (w_src, w_v),
                (m_src, m_v),
            ),
            sem,
            8,
        )
        begun[0].wait()

        def token_chunk(rows):
            xhat, _ = norm_parts(x_v[rows, :].astype(F32))
            h1_v[rows, :] = (xhat * gains_ref[0:1, :]).astype(BF16)

        row_chunks(x_v.shape[0], CHUNK, token_chunk)
        begun[1].wait()
        for t in range(4):
            cols = columns(512 * t, 512)
            kv_v[:, cols] = dot_nn(h1_v[...], wkv_v[:, cols]).astype(BF16)
        sent = start_all(((kv_v, kv_out), (h1_v, h1_out)), sem, 13)
        wait_all(begun[2:])

    @pl.when(flags_ref[0] == 1)
    def _():
        if first:
            c_v[...] = init_v[...].T
            begun_here = []
        else:
            begun_here = start_all(
                ((c_hbm, c_v), (w_src, w_v), (kv_hbm, kv_v), (m_src, m_v)), sem, 8
            )
            begun_here[0].wait()
        outs = start_all(((c_v, cs_hbm),), sem)

        def norm_chunk(rows):
            xhat, _ = norm_parts(c_v[rows, :].astype(F32))
            hc_v[rows, :] = (xhat * gains_ref[2:3, :]).astype(BF16)

        row_chunks(states, CHUNK, norm_chunk)
        outs += start_all(((hc_v, hc_hbm),), sem, 1)
        for copy in begun_here[1:2]:
            copy.wait()
        for t in range(6):
            cols = columns(512 * t, 512)
            product = dot_nn(hc_v[...], w_v[:, cols])
            ckvq_v[:, cols] = (product if t < 4 else product * Q_SCALE).astype(BF16)
        outs += start_all(((ckvq_v, ckvq_hbm),), sem, 2)
        wait_all(begun_here[2:])
        nvalid = flags_ref[1]
        allowed = row_iota(kv_v.shape[0], states) < nvalid

        def scores(h):
            q = ckvq_v[:, columns(2 * width + h * HEAD, HEAD)]
            return (
                dot_nt(ckvq_v[:, columns(h * HEAD, HEAD)], q),
                dot_nt(kv_v[:, columns(h * HEAD, HEAD)], q),
            )

        def soft(h, pair):
            return soft_forward(pair[0], jnp.where(allowed, pair[1], NEG))

        def mix(h, parts):
            one, two, factor, lse = parts
            mixed = dot_nn(ckvq_v[:, columns(width + h * HEAD, HEAD)].T, one)
            mixed += dot_nn(kv_v[:, columns(width + h * HEAD, HEAD)].T, two)
            upd_v[:, columns(h * HEAD, HEAD)] = (mixed * factor).T.astype(BF16)
            lse_v[h : h + 1, :] = lse

        pipeline(HEADS, scores, soft, mix)
        outs += start_all(((upd_v, upd_hbm), (lse_v, lse_hbm)), sem, 3)
        z_v[...] = dot_nn(upd_v[...], m_v[...])
        outs += start_all(((z_v, z_hbm),), sem, 5)

        def gate_chunk(rows):
            gate = gains_ref[3:4, :]
            new = gate * c_v[rows, :].astype(F32) + (1.0 - gate) * z_v[rows, :]
            new_v[rows, :] = new.astype(BF16)

        row_chunks(states, CHUNK, gate_chunk)
        outs += start_all(((new_v, new_hbm),), sem, 6)
        wait_all(outs)

    if first:
        wait_all(sent)


def advance(flags, gains, c, wa, kv, stash):
    states, width = c.shape
    rows = states if kv is None else kv.shape[0]
    first = stash is None
    extra = () if first else tuple(stash)
    shapes = [
        shape((states, width), BF16),
        shape((states, width), BF16),
        shape((states, width), BF16),
        shape((states, 3 * width), BF16),
        shape((states, width), BF16),
        shape((states, width), F32),
        shape((HEADS, states), F32),
    ]
    scratch = [
        pltpu.VMEM((states, width), BF16),
        pltpu.VMEM((width, 3 * width), BF16),
        pltpu.VMEM((width, width), BF16),
        pltpu.VMEM((rows, 2 * width), BF16),
        pltpu.VMEM((states, width), BF16),
        pltpu.VMEM((states, 3 * width), BF16),
        pltpu.VMEM((states, width), BF16),
        pltpu.VMEM((states, width), F32),
        pltpu.VMEM((states, width), BF16),
        pltpu.VMEM((HEADS, states), F32),
        pltpu.SemaphoreType.DMA((15,)),
    ]
    if first:
        kernel = lambda f, g, x, w, *refs: advance_kernel(True, f, g, x, w, None, *refs)
        shapes = [shape((rows, 2 * width), BF16), shape((rows, width), BF16)] + shapes
        scratch += [
            pltpu.VMEM((rows, width), BF16),
            pltpu.VMEM((width, 2 * width), BF16),
            pltpu.VMEM((rows, width), BF16),
            pltpu.VMEM((width, states), BF16),
        ]
        args = (flags, gains, c, wa)
    else:
        kernel = partial(advance_kernel, False)
        args = (flags, gains, c, wa, kv) + extra
    return pl.pallas_call(
        kernel,
        in_specs=[SMEM, VMEM] + [HBM] * (len(args) - 2),
        out_specs=[HBM] * len(shapes),
        out_shape=shapes,
        scratch_shapes=scratch,
        input_output_aliases={} if first else {5 + i: 1 + i for i in range(6)},
        compiler_params=pltpu.CompilerParams(vmem_limit_bytes=VMEM_LIMIT),
        cost_estimate=pl.CostEstimate(flops=9 << 30, bytes_accessed=24 * MIB, transcendentals=4 * MIB),
        name="advance",
    )(*args)


def bias_tiles(t_row):
    spread = jnp.broadcast_to(t_row, (128, t_row.shape[1]))
    grid = pltpu.roll(spread, 0, axis=1, stride=1, stride_axis=0)
    lane = lax.broadcasted_iota(jnp.int32, (128, 128), 1)
    sub = lax.broadcasted_iota(jnp.int32, (128, 128), 0)
    tiles = [grid[:, 128 * d : 128 * d + 128] for d in range(4)]
    tiles[0] = jnp.where(lane >= sub, tiles[0], NEG)
    return tiles


def bias_part(tiles, part):
    none = jnp.full((128, 128), NEG, F32)
    rows = []
    for j in range(2 * part + 2):
        row = [tiles[i - j] if i >= j else none for i in (2 * part, 2 * part + 1)]
        rows.append(jnp.concatenate(row, axis=1))
    return jnp.concatenate(rows, axis=0)


def token_kernel(flags_ref, t_ref, h1_hbm, kv_hbm, ckvq_hbm, wa_hbm, o_hbm, q_hbm, lse_hbm,
                 h1_v, q_v, kv_v, ckv_v, wq_v, o_v, lse_v, sem):
    width = h1_v.shape[1]
    half = HEADS // 2 * HEAD
    loads = [(h1_hbm, h1_v)]
    for s in range(2):
        here, there = pl.ds(s * half, half), pl.ds(width + s * half, half)
        loads += [
            (wa_hbm.at[:, pl.ds(A_Q + s * half, half)], wq_v.at[:, here]),
            (ckvq_hbm.at[:, here], ckv_v.at[:, here]),
            (kv_hbm.at[:, here], kv_v.at[:, here]),
            (ckvq_hbm.at[:, there], ckv_v.at[:, there]),
            (kv_hbm.at[:, there], kv_v.at[:, there]),
        ]
    begun = start_all(loads, sem)
    begun.pop(0).wait()
    nvalid = flags_ref[1]
    units = [(h, part) for h in range(HEADS) for part in range(2)]
    tile_cache = {}

    def tiles_of(h, key):
        if (h, key) not in tile_cache:
            tile_cache.clear()
            tile_cache[(h, key)] = bias_tiles(t_ref[h : h + 1, :])
        return tile_cache[(h, key)]

    def pick(n):
        h, part = units[n]
        return h, part, columns(256 * part, 256), 256 * (part + 1), columns(h * HEAD, HEAD), columns(width + h * HEAD, HEAD)

    def masked(scores, h, part, key):
        scores = scores + bias_part(tiles_of(h, key), part)
        return jnp.where(row_iota(scores.shape[0], 256) < nvalid, scores, NEG)

    def scores(n):
        h, part, span, used, here, there = pick(n)
        if part == 0 and h in (0, HEADS // 2):
            s = h // (HEADS // 2)
            wait_all(begun[5 * s :][:5])
            cols = columns(s * half, half)
            q_v[:, cols] = (dot_nn(h1_v[...], wq_v[:, cols]) * Q_SCALE).astype(BF16)
        q = q_v[span, here]
        return dot_nt(ckv_v[:, here], q), dot_nt(kv_v[:used, here], q)

    def soft(n, pair):
        h, part, span, used, here, there = pick(n)
        return soft_forward(pair[0], masked(pair[1], h, part, 0))

    def mix(n, parts):
        h, part, span, used, here, there = pick(n)
        one, two, factor, lse = parts
        mixed = dot_nn(ckv_v[:, there].T, one) + dot_nn(kv_v[:used, there].T, two)
        o_v[span, here] = (mixed * factor).T.astype(BF16)
        lse_v[h : h + 1, span] = lse

    pipeline(len(units), scores, soft, mix)
    wait_all(start_all(((o_v, o_hbm), (q_v, q_hbm), (lse_v, lse_hbm)), sem, 11))


def token_forward(flags, t, h1, kv, ckvq, wa):
    rows, width = h1.shape
    states = ckvq.shape[0]
    narrow = shape((rows, width), BF16)
    return pl.pallas_call(
        token_kernel,
        in_specs=[SMEM, VMEM] + [HBM] * 4,
        out_specs=[HBM] * 3,
        out_shape=[narrow, narrow, shape((HEADS, rows), F32)],
        scratch_shapes=[
            pltpu.VMEM((rows, width), BF16),
            pltpu.VMEM((rows, width), BF16),
            pltpu.VMEM((rows, 2 * width), BF16),
            pltpu.VMEM((states, 2 * width), BF16),
            pltpu.VMEM((width, width), BF16),
            pltpu.VMEM((rows, width), BF16),
            pltpu.VMEM((HEADS, rows), F32),
            pltpu.SemaphoreType.DMA((14,)),
        ],
        compiler_params=pltpu.CompilerParams(vmem_limit_bytes=VMEM_LIMIT),
        cost_estimate=pl.CostEstimate(flops=4 << 30, bytes_accessed=10 * MIB, transcendentals=4 * MIB),
        name="token_forward",
    )(flags, t, h1, kv, ckvq, wa)


def block_kernel(flags_ref, t_ref, gains_ref, x_hbm, g_hbm, o_hbm, q_hbm, lse_hbm, kv_hbm, ckvq_hbm, wb_hbm,
                 x1_hbm, h2_hbm, act_hbm, dup_hbm, dx1_hbm, da_hbm, dq_hbm, dkv_hbm, dst_hbm,
                 db_ref, sums_ref,
                 x_v, g_v, q_v, kv_v, ckv_v, wo_v, wu_v, wd_v, o_v, x1_v, h2_v, act_v, dup_v,
                 dh_v, do_v, dq_v, dkv_v, dst_v, lse_v, sem):
    rows, width = x_v.shape
    half = HEADS // 2 * HEAD
    loads = [
        (o_hbm, o_v),
        (wb_hbm.at[:, pl.ds(W_OUT, width)], wo_v),
        (x_hbm, x_v),
        (g_hbm, g_v),
        *[
            (wb_hbm.at[:, pl.ds(base + s * width, width)], ref.at[:, pl.ds(s * width, width)])
            for s in range(4)
            for base, ref in ((W_UP, wu_v), (W_DOWN, wd_v))
        ],
        (q_hbm, q_v),
        (ckvq_hbm.at[:, pl.ds(0, 2 * width)], ckv_v),
        (kv_hbm, kv_v),
        (lse_hbm, lse_v),
    ]
    begun = start_all(loads, sem)
    nvalid = flags_ref[1]
    units = [(h, part) for h in range(HEADS) for part in range(2)]
    tile_cache = {}

    def tiles_of(h, key):
        if (h, key) not in tile_cache:
            tile_cache.clear()
            tile_cache[(h, key)] = bias_tiles(t_ref[h : h + 1, :])
        return tile_cache[(h, key)]

    def pick(n):
        h, part = units[n]
        return h, part, columns(256 * part, 256), 256 * (part + 1), columns(h * HEAD, HEAD), columns(width + h * HEAD, HEAD)

    def masked(scores, h, part, key):
        scores = scores + bias_part(tiles_of(h, key), part)
        return jnp.where(row_iota(scores.shape[0], 256) < nvalid, scores, NEG)

    wait_all(begun[:3])
    x1_v[...] = x_v[...].astype(F32) + dot_nn(o_v[...], wo_v[...])

    def norm_chunk(span):
        xhat, _ = norm_parts(x1_v[span, :])
        h2_v[span, :] = (xhat * gains_ref[1:2, :]).astype(BF16)

    row_chunks(rows, CHUNK, norm_chunk)
    outs = start_all(((x1_v, x1_hbm), (h2_v, h2_hbm)), sem, 20)
    begun[3].wait()

    tile = 512

    def hidden(i):
        if i % 2 == 0:
            wait_all(begun[4 + i : 6 + i])
        slab = wd_v[columns(tile * (i % 2), tile), columns(width * (i // 2), width)]
        return dot_nn(h2_v[...], wu_v[:, columns(tile * i, tile)]), dot_nt(g_v[...], slab)

    def activate(i, pair):
        up, dact = pair
        root = 0.7978845608028654
        square = up * up
        th = jnp.tanh(up * (root + (root * 0.044715) * square))
        part = 0.5 + 0.5 * th
        slope = part + up * (part - part * part) * (2 * root + (6 * root * 0.044715) * square)
        act_v[:, columns(tile * i, tile)] = (up * part).astype(BF16)
        dup_v[:, columns(tile * i, tile)] = (dact * slope).astype(BF16)

    pipeline(4 * width // tile, hidden, activate, lambda i, nothing: None)
    outs += start_all(((act_v, act_hbm), (dup_v, dup_hbm)), sem, 23)
    dh_v[...] = dot_nt(dup_v[...], wu_v[...])
    sums_ref[...] = jnp.zeros_like(sums_ref)

    def back_chunk(span):
        dx, gain_term = norm_back(x1_v[span, :], gains_ref[1:2, :], dh_v[span, :])
        dx = dx + g_v[span, :].astype(F32)
        dh_v[span, :] = dx
        x_v[span, :] = dx.astype(BF16)
        sums_ref[0:1, :] += jnp.sum(gain_term, axis=0, keepdims=True)

    row_chunks(rows, CHUNK, back_chunk)
    outs += start_all(((dh_v, dx1_hbm), (x_v, da_hbm)), sem, 25)
    do_v[...] = dot_nt(x_v[...], wo_v[...]).astype(BF16)

    wait_all(begun[12:])
    held = {}

    def back_scores(n):
        h, part, span, used, here, there = pick(n)
        q, do = q_v[span, here], do_v[span, here]
        return (
            dot_nt(ckv_v[:, here], q),
            dot_nt(kv_v[:used, here], q),
            dot_nt(ckv_v[:, there], do),
            dot_nt(kv_v[:used, there], do),
        )

    def back_soft(n, parts):
        h, part, span, used, here, there = pick(n)
        lse = lse_v[h : h + 1, span]
        p1, p2, d1, d2 = soft_backward(
            parts[0], masked(parts[1], h, part, 1), parts[2], parts[3], lse
        )
        shear = held.setdefault(("shear", h), [0.0] * 4)
        for j in range(2 * part + 2):
            for i in (0, 1):
                d = 2 * part + i - j
                if d >= 0:
                    shear[d] = shear[d] + d2[128 * j : 128 * j + 128, 128 * i : 128 * i + 128]
        if part == 1:
            grid = jnp.concatenate(held.pop(("shear", h)), axis=1)
            size = grid.shape[1]
            flipped = grid[:8]
            for group in range(1, 16):
                flipped += pltpu.roll(grid[8 * group : 8 * group + 8], size - 8 * group, axis=1)
            for step in (1, 2, 4):
                moved = pltpu.roll(flipped, size - step, axis=1)
                flipped = jnp.where((row_iota(8, size) // step) % 2 == 1, moved, flipped)
            db_ref[h : h + 1, :] = jnp.sum(flipped, axis=0, keepdims=True)
        return p1, p2, d1.astype(BF16), d2.astype(BF16)

    def back_mix(n, parts):
        h, part, span, used, here, there = pick(n)
        p1, p2, d1, d2 = parts
        q, do = q_v[span, here], do_v[span, here]
        terms = [dot_nn(d1, q), dot_nn(p1, do), dot_nn(d2, q), dot_nn(p2, do)]
        dqt = dot_nn(ckv_v[:, here].T, d1) + dot_nn(kv_v[:used, here].T, d2)
        dq_v[span, here] = (dqt.T * SCALE).astype(BF16)
        if part == 0:
            held[("terms", h)] = terms
            return
        before = held.pop(("terms", h))
        dst_v[:, here] = ((before[0] + terms[0]) * (1.0 / LOG2E)).astype(BF16)
        dst_v[:, there] = (before[1] + terms[1]).astype(BF16)
        dkv_v[:256, here] = ((before[2] + terms[2][:256]) * (1.0 / LOG2E)).astype(BF16)
        dkv_v[256:, here] = (terms[2][256:] * (1.0 / LOG2E)).astype(BF16)
        dkv_v[:256, there] = (before[3] + terms[3][:256]).astype(BF16)
        dkv_v[256:, there] = terms[3][256:].astype(BF16)

    pipeline(len(units), back_scores, back_soft, back_mix)
    outs += start_all(((dq_v, dq_hbm), (dkv_v, dkv_hbm), (dst_v, dst_hbm)), sem, 27)
    wait_all(outs)


def block_part(flags, t, gains, x, g, o, q, lse, kv, ckvq, wb):
    rows, width = x.shape
    states = ckvq.shape[0]
    hidden = 4 * width
    narrow, wide = shape((rows, width), BF16), shape((rows, width), F32)
    return pl.pallas_call(
        block_kernel,
        in_specs=[SMEM, VMEM, VMEM] + [HBM] * 8,
        out_specs=[HBM] * 9 + [VMEM] * 2,
        out_shape=[
            wide,
            narrow,
            shape((rows, hidden), BF16),
            shape((rows, hidden), BF16),
            wide,
            narrow,
            narrow,
            shape((rows, 2 * width), BF16),
            shape((states, 2 * width), BF16),
            shape((HEADS, rows), F32),
            shape((8, width), F32),
        ],
        scratch_shapes=[
            pltpu.VMEM((rows, width), BF16),
            pltpu.VMEM((rows, width), BF16),
            pltpu.VMEM((rows, width), BF16),
            pltpu.VMEM((rows, 2 * width), BF16),
            pltpu.VMEM((states, 2 * width), BF16),
            pltpu.VMEM((width, width), BF16),
            pltpu.VMEM((width, hidden), BF16),
            pltpu.VMEM((width, hidden), BF16),
            pltpu.VMEM((rows, width), BF16),
            pltpu.VMEM((rows, width), F32),
            pltpu.VMEM((rows, width), BF16),
            pltpu.VMEM((rows, hidden), BF16),
            pltpu.VMEM((rows, hidden), BF16),
            pltpu.VMEM((rows, width), F32),
            pltpu.VMEM((rows, width), BF16),
            pltpu.VMEM((rows, width), BF16),
            pltpu.VMEM((rows, 2 * width), BF16),
            pltpu.VMEM((states, 2 * width), BF16),
            pltpu.VMEM((HEADS, rows), F32),
            pltpu.SemaphoreType.DMA((31,)),
        ],
        compiler_params=pltpu.CompilerParams(vmem_limit_bytes=VMEM_LIMIT),
        cost_estimate=pl.CostEstimate(flops=25 << 30, bytes_accessed=40 * MIB, transcendentals=10 * MIB),
        name="block_part",
    )(flags, t, gains, x, g, o, q, lse, kv, ckvq, wb)


def retreat_kernel(first, looped, flags_ref, gains_ref, lam_hbm, wa_hbm, kv_hbm, cs_hbm, ckvq_hbm, z_hbm,
                   lse_hbm, dst_hbm, *refs):
    if not first:
        refs = refs[4:]
    (prev_hbm, dz_hbm, dcs_hbm, dkv_hbm, sums_hbm) = refs[:5]
    (lam_v, w_v, m_v, kv_v, c_v, ckvq_v, z_v, lse_v, dst_v,
     dz_v, du_v, dcs_v, dkv_v, dh_v, prev_v, sums_v, sem) = refs[5:]
    states, width = c_v.shape

    @pl.when(flags_ref[0] == 1)
    def _():
        begun = start_all(
            (
                (lam_hbm, lam_v),
                (cs_hbm, c_v),
                (z_hbm, z_v),
                (wa_hbm.at[:, pl.ds(A_MERGE, width)], m_v),
                (ckvq_hbm, ckvq_v),
                (kv_hbm, kv_v),
                (lse_hbm, lse_v),
                (dst_hbm, dst_v),
                (wa_hbm.at[:, pl.ds(A_STATE, 3 * width)], w_v),
            ),
            sem,
        )
        wait_all(begun[:3])
        sums_v[...] = jnp.zeros_like(sums_v)

        def gate_chunk(rows):
            lam = lam_v[rows, :].astype(F32)
            dz_v[rows, :] = ((1.0 - gains_ref[3:4, :]) * lam).astype(BF16)
            change = lam * (c_v[rows, :].astype(F32) - z_v[rows, :])
            sums_v[1:2, :] += jnp.sum(change, axis=0, keepdims=True)

        row_chunks(states, CHUNK, gate_chunk)
        outs = start_all(((dz_v, dz_hbm),), sem, 9)
        begun[3].wait()
        du_v[...] = dot_nt(dz_v[...], m_v[...]).astype(BF16)
        wait_all(begun[4:8])
        allowed = row_iota(kv_v.shape[0], states) < flags_ref[1]

        def pick(h):
            starts = [base + h * HEAD for base in (0, width, 2 * width)]
            return [pl.ds(pl.multiple_of(n, HEAD) if looped else n, HEAD) for n in starts]

        def scores(h):
            here, there, third = pick(h)
            q, du = ckvq_v[:, third], du_v[:, here]
            return (
                dot_nt(ckvq_v[:, here], q),
                dot_nt(kv_v[:, here], q),
                dot_nt(ckvq_v[:, there], du),
                dot_nt(kv_v[:, there], du),
            )

        def soft(h, parts):
            one, two, done, dtwo = parts
            two = jnp.where(allowed, two, NEG)
            p1, p2, d1, d2 = soft_backward(one, two, done, dtwo, lse_v[pl.ds(h, 1), :])
            return p1, p2, d1.astype(BF16), d2.astype(BF16)

        def mix(h, parts):
            here, there, third = pick(h)
            p1, p2, d1, d2 = parts
            q, du = ckvq_v[:, third], du_v[:, here]
            ln2 = 1.0 / LOG2E
            dcs_v[:, here] = (dot_nn(d1, q) * ln2 + dst_v[:, here].astype(F32)).astype(BF16)
            dcs_v[:, there] = (dot_nn(p1, du) + dst_v[:, there].astype(F32)).astype(BF16)
            dkv_v[:, here] = (dot_nn(d2, q) * ln2).astype(BF16)
            dkv_v[:, there] = dot_nn(p2, du).astype(BF16)
            dqt = dot_nn(ckvq_v[:, here].T, d1) + dot_nn(kv_v[:, here].T, d2)
            dcs_v[:, third] = (dqt.T * SCALE).astype(BF16)

        def some(block, carry):
            base = 2 * block
            pipeline(2, lambda h: scores(base + h), lambda h, p: soft(base + h, p), lambda h, p: mix(base + h, p))
            return carry

        if looped:
            lax.fori_loop(0, HEADS // 2, some, 0)
        else:
            pipeline(HEADS, scores, soft, mix)
        outs += start_all(((dcs_v, dcs_hbm), (dkv_v, dkv_hbm)), sem, 10)
        begun[8].wait()
        dh_v[...] = dot_nt(dcs_v[...], w_v[...])

        def norm_chunk(rows):
            dx, gain_term = norm_back(c_v[rows, :].astype(F32), gains_ref[2:3, :], dh_v[rows, :])
            prev = dx + gains_ref[3:4, :] * lam_v[rows, :].astype(F32)
            prev_v[rows, :] = prev.astype(BF16)
            sums_v[0:1, :] += jnp.sum(gain_term, axis=0, keepdims=True)

        row_chunks(states, CHUNK, norm_chunk)
        outs += start_all(((prev_v, prev_hbm), (sums_v, sums_hbm)), sem, 12)
        wait_all(outs)


def retreat(flags, gains, lam, wa, kv, cs, ckvq, z, lse, dst, stash, looped):
    states, width = cs.shape
    rows = kv.shape[0]
    first = stash is None
    extra = () if first else tuple(stash)
    out = pl.pallas_call(
        partial(retreat_kernel, first, looped),
        in_specs=[SMEM, VMEM] + [HBM] * (8 + len(extra)),
        out_specs=[HBM] * 5,
        out_shape=[
            shape((states, width), BF16),
            shape((states, width), BF16),
            shape((states, 3 * width), BF16),
            shape((rows, 2 * width), BF16),
            shape((8, width), F32),
        ],
        scratch_shapes=[
            pltpu.VMEM((states, width), lam.dtype),
            pltpu.VMEM((width, 3 * width), BF16),
            pltpu.VMEM((width, width), BF16),
            pltpu.VMEM((rows, 2 * width), BF16),
            pltpu.VMEM((states, width), BF16),
            pltpu.VMEM((states, 3 * width), BF16),
            pltpu.VMEM((states, width), F32),
            pltpu.VMEM((HEADS, states), F32),
            pltpu.VMEM((states, 2 * width), BF16),
            pltpu.VMEM((states, width), BF16),
            pltpu.VMEM((states, width), BF16),
            pltpu.VMEM((states, 3 * width), BF16),
            pltpu.VMEM((rows, 2 * width), BF16),
            pltpu.VMEM((states, width), F32),
            pltpu.VMEM((states, width), BF16),
            pltpu.VMEM((8, width), F32),
            pltpu.SemaphoreType.DMA((14,)),
        ],
        input_output_aliases={} if first else {10 + i: 1 + i for i in range(4)},
        compiler_params=pltpu.CompilerParams(vmem_limit_bytes=VMEM_LIMIT),
        cost_estimate=pl.CostEstimate(flops=13 << 30, bytes_accessed=32 * MIB, transcendentals=4 * MIB),
        name="retreat",
    )(flags, gains, lam, wa, kv, cs, ckvq, z, lse, dst, *extra)
    return out[0], list(out[1:])


def input_grad_kernel(gains_ref, x_hbm, dx1_hbm, dq_hbm, one_hbm, two_hbm, wa_hbm, out_hbm, sums_ref,
                      x_v, dx_v, dq_v, one_v, two_v, wkv_v, wq_v, dh_v, sem):
    rows, width = x_v.shape
    begun = start_all(
        (
            (one_hbm, one_v),
            (two_hbm, two_v),
            (wa_hbm.at[:, pl.ds(A_KV, 2 * width)], wkv_v),
            (dq_hbm, dq_v),
            (wa_hbm.at[:, pl.ds(A_Q, width)], wq_v),
            (x_hbm, x_v),
            (dx1_hbm, dx_v),
        ),
        sem,
    )
    wait_all(begun[:2])
    one_v[...] = (one_v[...].astype(F32) + two_v[...].astype(F32)).astype(BF16)
    begun[2].wait()
    dh_v[...] = dot_nt(one_v[...], wkv_v[...])
    wait_all(begun[3:5])
    dh_v[...] += dot_nt(dq_v[...], wq_v[...])
    wait_all(begun[5:])
    sums_ref[...] = jnp.zeros_like(sums_ref)

    def chunk(span):
        dx, gain_term = norm_back(x_v[span, :].astype(F32), gains_ref[0:1, :], dh_v[span, :])
        dx_v[span, :] += dx
        sums_ref[0:1, :] += jnp.sum(gain_term, axis=0, keepdims=True)

    row_chunks(rows, CHUNK, chunk)
    pltpu.sync_copy(dx_v, out_hbm)


def input_grad(gains, x, dx1, dq, one, two, wa):
    rows, width = x.shape
    return pl.pallas_call(
        input_grad_kernel,
        in_specs=[VMEM] + [HBM] * 6,
        out_specs=[HBM, VMEM],
        out_shape=[shape((rows, width), F32), shape((8, width), F32)],
        scratch_shapes=[
            pltpu.VMEM((rows, width), BF16),
            pltpu.VMEM((rows, width), F32),
            pltpu.VMEM((rows, width), BF16),
            pltpu.VMEM((rows, 2 * width), BF16),
            pltpu.VMEM((rows, 2 * width), BF16),
            pltpu.VMEM((width, 2 * width), BF16),
            pltpu.VMEM((width, width), BF16),
            pltpu.VMEM((rows, width), F32),
            pltpu.SemaphoreType.DMA((7,)),
        ],
        compiler_params=pltpu.CompilerParams(vmem_limit_bytes=VMEM_LIMIT),
        cost_estimate=NO_COST,
        name="input_grad",
    )(gains, x, dx1, dq, one, two, wa)


def dot_tn(a, b):
    return lax.dot_general(a, b, (((0,), (0,)), ((), ())), preferred_element_type=F32)


def early_kernel(share, fresh, flags_ref, o_hbm, da_hbm, h1_hbm, dq_hbm, h2_hbm, dup_hbm, act_hbm, g_hbm, *refs):
    outs = refs[:-11] if fresh else refs[(len(refs) - 11) // 2 : -11]
    (o_v, da_v, h1_v, dq_v, h2_v, g_v, dup_v, act_v, tile_v, sem, out_sem) = refs[-11:]
    width = h2_v.shape[1]
    tile = tile_v.shape[-1]
    cut = B_END // 2
    mine = flags_ref[2]

    @pl.when(flags_ref[0] == 1)
    def _():
        begun = start_all(
            ((act_hbm, act_v), (g_hbm, g_v), (o_hbm, o_v), (da_hbm, da_v), (h1_hbm, h1_v), (dq_hbm, dq_v),
             (h2_hbm, h2_v), (dup_hbm, dup_v)), sem)

        def outgoing(slot, base, n):
            here = pl.multiple_of(base % cut + n * tile, tile)
            if share % 32:
                there = pl.ds(pl.multiple_of(base + n * tile, tile), tile)
                pairs = [(tile_v.at[slot], outs[0].at[:, there])]
            else:
                send, keep = outs[2 * (base // cut) : 2 * (base // cut) + 2]
                pairs = [
                    (tile_v.at[slot, :, 1 - mine], send.at[:, :, pl.ds(here, tile)]),
                    (tile_v.at[slot, :, mine], keep.at[:, :, pl.ds(here, tile)]),
                ]
            return [pltpu.make_async_copy(src, dst, out_sem.at[slot, m]) for m, (src, dst) in enumerate(pairs)]

        def emit(count, base, product, done):
            def step(n, carry):
                slot = n % 2
                copies = outgoing(slot, base, n)
                value = product(n).astype(BF16)

                @pl.when(n + done >= 2)
                def _():
                    wait_all(copies)

                tile_v[slot] = value.reshape(tile_v.shape[1:])
                for copy in copies:
                    copy.start()
                return carry

            lax.fori_loop(0, count, step, 0)

        def at(n):
            return pl.ds(pl.multiple_of(n * tile, tile), tile)

        def down(n):
            slab = pl.ds(pl.multiple_of((n // 2) * width, width), width)
            return dot_tn(act_v[:, slab], g_v[:, at(n % 2)])

        first = (cut - B_UP) // tile
        wait_all(begun[:2])
        emit(8, B_DOWN, down, 0)
        wait_all(begun[2:4])
        emit(2, B_OUT, lambda n: dot_tn(o_v[...], da_v[:, at(n)]), 8)
        wait_all(begun[4:6])
        emit(2, B_Q, lambda n: dot_tn(h1_v[...], dq_v[:, at(n)]), 10)
        wait_all(begun[6:8])
        emit(first, B_UP, lambda n: dot_tn(h2_v[...], dup_v[:, at(n)]), 12)
        emit(8 - first, cut, lambda n: dot_tn(h2_v[...], dup_v[:, at(n + first)]), 12 + first)
        for slot in range(2):
            wait_all(outgoing(slot, 0, 0))


def early_grads(flags, share, before, o, da, h1, dq, h2, dup, act, g):
    rows, width = o.shape
    pairs = width // (2 * share)
    if share % 32:
        outs = [shape((width, B_END), BF16)]
        tiles = pltpu.VMEM((2, width, 512), BF16)
    else:
        outs = [shape((pairs, share, B_END // 2), BF16)] * 4
        tiles = pltpu.VMEM((2, pairs, 2, share, 512), BF16)
    narrow = pltpu.VMEM((rows, width), BF16)
    wide = pltpu.VMEM((rows, 4 * width), BF16)
    return pl.pallas_call(
        partial(early_kernel, share, not before),
        in_specs=[SMEM] + [HBM] * (8 + len(before)),
        out_specs=[HBM] * len(outs),
        out_shape=outs,
        scratch_shapes=[narrow] * 6 + [wide] * 2 + [tiles, pltpu.SemaphoreType.DMA((8,)), pltpu.SemaphoreType.DMA((2, 2))],
        input_output_aliases={9 + n: n for n in range(len(before))},
        compiler_params=pltpu.CompilerParams(vmem_limit_bytes=VMEM_LIMIT),
        cost_estimate=pl.CostEstimate(flops=11 << 30, bytes_accessed=34 * MIB, transcendentals=0),
        name="early_grads",
    )(flags, o, da, h1, dq, h2, dup, act, g, *before)


def layer_out_kernel(x1_ref, act_ref, wd_ref, out_ref, acc_ref):
    i = pl.program_id(0)
    term = dot_nn(act_ref[...], wd_ref[...])

    @pl.when(i == 0)
    def _():
        acc_ref[...] = x1_ref[...] + term

    @pl.when(i > 0)
    def _():
        acc_ref[...] += term

    @pl.when(i == pl.num_programs(0) - 1)
    def _():
        out_ref[...] = acc_ref[...].astype(BF16)


def layer_output(x1, act, wb):
    rows, width = x1.shape
    return pl.pallas_call(
        layer_out_kernel,
        grid=(4,),
        in_specs=[
            pl.BlockSpec((rows, width), lambda i: (0, 0)),
            pl.BlockSpec((rows, width), lambda i: (0, i)),
            pl.BlockSpec((width, width), lambda i: (0, W_DOWN // width + i)),
        ],
        out_specs=pl.BlockSpec((rows, width), lambda i: (0, 0)),
        out_shape=shape((rows, width), BF16),
        scratch_shapes=[pltpu.VMEM((rows, width), F32)],
        compiler_params=pltpu.CompilerParams(vmem_limit_bytes=VMEM_LIMIT),
        cost_estimate=pl.CostEstimate(flops=4 << 30, bytes_accessed=15 * MIB, transcendentals=0),
        name="layer_output",
    )(x1, act, wb)


def late_kernel(plan, share, flags_ref, *refs):
    count = len(refs) - 2
    send_ref, keep_ref = refs[count:]
    mine = flags_ref[2] == 0
    tile = 512
    for n, (kind, a, b) in enumerate(plan):
        if kind == "product":
            value = dot_tn(refs[a][...], refs[b[0]][:, columns(b[1], tile)])
        elif kind == "sum":
            total = sum(refs[m][:, columns(b[1], tile)].astype(F32) for m in b[0])
            value = dot_tn(refs[a][...], total.astype(BF16))
        else:
            value = jnp.where(flags_ref[3] == 0, refs[a][...].T.astype(F32), 0.0)
        value = value.astype(BF16)
        cols = columns(n * tile, tile)
        for m in range(value.shape[0] // (2 * share)):
            low = value[2 * share * m : 2 * share * m + share]
            high = value[2 * share * m + share : 2 * share * (m + 1)]
            rows = columns(share * m, share)
            send_ref[rows, cols] = jnp.where(mine, high, low)
            keep_ref[rows, cols] = jnp.where(mine, low, high)


def late_whole_kernel(plan, flags_ref, *refs):
    tile = 512
    for n, (kind, a, b) in enumerate(plan):
        if kind == "product":
            value = dot_tn(refs[a][...], refs[b[0]][:, columns(b[1], tile)])
        elif kind == "sum":
            total = sum(refs[m][:, columns(b[1], tile)].astype(F32) for m in b[0])
            value = dot_tn(refs[a][...], total.astype(BF16))
        else:
            value = jnp.where(flags_ref[3] == 0, refs[a][...].T.astype(F32), 0.0)
        refs[-1][:, columns(n * tile, tile)] = value.astype(BF16)


def late_grads(flags, share, plan, *arrays):
    width = arrays[0].shape[1]
    cols = 512 * len(plan)
    params = dict(
        in_specs=[SMEM] + [VMEM] * len(arrays),
        compiler_params=pltpu.CompilerParams(vmem_limit_bytes=VMEM_LIMIT),
        cost_estimate=NO_COST,
        name="late_grads",
    )
    if share % 32:
        whole = pl.pallas_call(
            partial(late_whole_kernel, plan), out_specs=VMEM, out_shape=shape((width, cols), BF16), **params
        )(flags, *arrays)
        blocks = whole.reshape(width // (2 * share), 2, share, cols)
        keep = lax.dynamic_index_in_dim(blocks, flags[2], 1, keepdims=False)
        send = lax.dynamic_index_in_dim(blocks, 1 - flags[2], 1, keepdims=False)
        return send, keep
    half = shape((width // 2, cols), BF16)
    send, keep = pl.pallas_call(
        partial(late_kernel, plan, share), out_specs=[VMEM] * 2, out_shape=[half, half], **params
    )(flags, *arrays)
    dims = (width // (2 * share), share, cols)
    return send.reshape(dims), keep.reshape(dims)


def settle_kernel(devices, in_ref, q_ref, out_ref, up_ref, down_ref):
    share = in_ref.shape[0]
    width = share * devices
    q_ref[...] = in_ref[:, columns(B_Q, width)].astype(F32)
    out_ref[...] = in_ref[:, columns(B_OUT, width)].astype(F32)
    for d in range(devices):
        pieces = [in_ref[:, columns(B_UP + s * width + d * share, share)] for s in range(4)]
        up_ref[:, columns(4 * share * d, 4 * share)] = jnp.concatenate(pieces, axis=1).astype(F32)
    for s in range(4):
        down_ref[columns(s * share, share), :] = in_ref[:, columns(B_DOWN + s * width, width)].astype(F32)


def settle(early, devices):
    share = early.shape[0]
    width = share * devices
    return pl.pallas_call(
        partial(settle_kernel, devices),
        in_specs=[VMEM],
        out_specs=[VMEM] * 4,
        out_shape=[
            shape((share, width), F32),
            shape((share, width), F32),
            shape((share, 4 * width), F32),
            shape((4 * share, width), F32),
        ],
        compiler_params=pltpu.CompilerParams(vmem_limit_bytes=VMEM_LIMIT),
        name="settle",
    )(early)


def orders_of(devices):
    bits = [1 << n for n in range(devices.bit_length() - 1)]
    if devices != 32:
        return [bits] * 2, [bits] * 2
    core, x, y, z, far = bits
    return [[core, y, z, x, far], [core, z, y, x, far]], [[core, y, x, z, far], [core, z, y, x, far]]


def exchange(value, bit, devices):
    return lax.ppermute(value, AXES, [(i, i ^ bit) for i in range(devices)])


def split_blocks(term, place, which):
    blocks, rows, cols = term.shape
    low = 1 << place
    view = term.reshape(blocks // (2 * low), 2, low, rows, cols)
    return lax.dynamic_index_in_dim(view, which, 1, keepdims=False).reshape(blocks // 2, rows, cols)


def half_kernel(count, which_ref, *refs):
    pairs, outs = refs[: 2 * count], refs[2 * count : 3 * count]
    scratch, (sem, out_sem) = refs[3 * count : 5 * count], refs[5 * count :]
    loads, stores = [], []
    for n in range(count):
        which = which_ref[n]
        loads.append(
            start_all(
                [(pairs[2 * n + m].at[:, which], scratch[2 * n + m]) for m in range(2)], sem, 2 * n
            )
        )
    for n in range(count):
        wait_all(loads[n])
        one, two = scratch[2 * n], scratch[2 * n + 1]
        high, low = one.shape[:2]

        def add(i, carry, one=one, two=two, low=low):
            one[i // low, i % low] = (
                one[i // low, i % low].astype(F32) + two[i // low, i % low].astype(F32)
            ).astype(BF16)
            return carry

        lax.fori_loop(0, high * low, add, 0)
        stores += start_all([(one, outs[n])], out_sem, n)
    wait_all(stores)


def half_sums(terms, places, which):
    share = terms[0][0].shape[1]
    if share % 32:
        return [
            sum(split_blocks(t, place, w).astype(F32) for t in pair).astype(BF16)
            for pair, place, w in zip(terms, places, which)
        ]
    args, outs, scratch = [], [], []
    for pair, place in zip(terms, places):
        blocks, rows, cols = pair[0].shape
        low = 1 << place
        high = blocks // (2 * low)
        args += [t.reshape(high, 2, low, rows, cols) for t in pair]
        outs.append(shape((high, low, rows, cols), BF16))
        scratch += [pltpu.VMEM((high, low, rows, cols), BF16)] * 2
    count = len(terms)
    results = pl.pallas_call(
        partial(half_kernel, count),
        in_specs=[SMEM] + [HBM] * (2 * count),
        out_specs=[HBM] * count,
        out_shape=outs,
        scratch_shapes=scratch + [pltpu.SemaphoreType.DMA((2 * count,)), pltpu.SemaphoreType.DMA((count,))],
        compiler_params=pltpu.CompilerParams(vmem_limit_bytes=VMEM_LIMIT),
        cost_estimate=NO_COST,
        name="half_sums",
    )(jnp.stack(which), *args)
    return [r.reshape(-1, *r.shape[2:]) for r in results]


class Stream:
    def __init__(self, send, keep, order, devices):
        self.devices, self.order, self.left = devices, list(order), sorted(order)
        self.keep, self.send, self.got = keep, send, None
        self.bit = self.order.pop(0)
        self.left.remove(self.bit)

    def move(self):
        self.got = exchange(self.send, self.bit, self.devices)
        self.send = None

    def result(self):
        return (self.keep.astype(F32) + self.got.astype(F32))[0]


class Few:
    def __init__(self, value, order, devices):
        self.devices, self.order, self.left, self.total = devices, list(order), sorted(order), value.astype(F32)
        self.pick()

    def pick(self):
        me = lax.axis_index(AXES)
        bits, self.order = self.order[:2], self.order[2:]
        masks = [0]
        for bit in bits:
            masks += [mask | bit for mask in masks]
        parts = []
        for mask in masks:
            value, left = self.total, list(self.left)
            for bit in bits:
                value = split_blocks(value, left.index(bit), ((me ^ mask) // bit) % 2)
                left.remove(bit)
            parts.append(value)
        self.left = [bit for bit in self.left if bit not in bits]
        self.keep, self.send, self.masks = parts[0], [part.astype(BF16) for part in parts[1:]], masks[1:]

    def move(self):
        self.got = [exchange(send, mask, self.devices) for send, mask in zip(self.send, self.masks)]
        self.send = None

    def split(self):
        self.total = self.keep + sum(got.astype(F32) for got in self.got)
        self.pick()

    def result(self):
        return (self.keep + sum(got.astype(F32) for got in self.got))[0]


class Step:
    def __init__(self, streams):
        self.streams, self.terms, self.places, self.mine = streams, [], [], []
        for stream in streams:
            stream.bit = stream.order.pop(0)
            self.places.append(stream.left.index(stream.bit))
            stream.left.remove(stream.bit)
            self.mine.append((lax.axis_index(AXES) // stream.bit) % 2)
            self.terms.append((stream.keep, stream.got))
        sends = half_sums(self.terms, self.places, [1 - m for m in self.mine])
        for stream, send in zip(streams, sends):
            stream.send = send

    def keep(self, after):
        after, self.terms = lax.optimization_barrier((after, self.terms))
        keeps = half_sums(self.terms, self.places, self.mine)
        for stream, keep in zip(self.streams, keeps):
            stream.keep = keep
        return after


def split(streams):
    step = Step(streams)
    sends = step.keep([stream.send for stream in streams])
    for stream, send in zip(streams, sends):
        stream.send = send


def body(
    layer_input,
    segment_length,
    output_gradient,
    state_cotangent,
    query_key_value_weight,
    state_key_value_weight,
    state_query_weight,
    output_weight,
    merge_weight,
    up_weight,
    down_weight,
    initial_state_learned,
    attention_norm_gain,
    feedforward_norm_gain,
    state_norm_gain,
    state_gate_logits,
    relative_position_bias,
):
    _, rows, width = layer_input.shape
    place = lax.axis_index("seq")
    count = lax.axis_size("seq")
    devices = count * lax.axis_size("dp")
    share = width // devices
    pairs = lax.axis_size("dp")

    bias_local = relative_position_bias.shape[0]
    small = jnp.stack(
        [
            attention_norm_gain,
            feedforward_norm_gain,
            state_norm_gain,
            state_gate_logits,
            jnp.pad(relative_position_bias, (0, share - bias_local)),
        ],
        axis=1,
    )
    small = jnp.pad(small, ((0, 0), (0, A_END - A_VEC - 5)))
    wa = jnp.concatenate(
        [
            query_key_value_weight[:, width:],
            state_key_value_weight,
            state_query_weight,
            merge_weight,
            initial_state_learned.T,
            query_key_value_weight[:, :width],
            small,
        ],
        axis=1,
    )
    up_local = up_weight.reshape(share, devices, 4, share).transpose(0, 2, 1, 3)
    down_local = down_weight.reshape(4, share, width).transpose(1, 0, 2)
    wb = jnp.concatenate(
        [
            output_weight,
            up_local.reshape(share, 4 * width),
            down_local.reshape(share, 4 * width),
        ],
        axis=1,
    )
    wa = lax.all_gather(wa, AXES, axis=0, tiled=True)
    wb = lax.all_gather(wb, AXES, axis=0, tiled=True)

    vectors = wa[:, A_VEC : A_VEC + 5].astype(F32).T
    gate = jax.nn.sigmoid(vectors[3:4])
    gains = jnp.concatenate([vectors[:3], gate, jnp.zeros((4, width), F32)], axis=0)
    table = vectors[4].reshape(devices, share)[:, :bias_local].reshape(HEADS, BUCKETS)
    onehot = np.eye(BUCKETS, dtype=np.float32)[:, bucket_of(rows)]
    t = jnp.dot(table * LOG2E, jnp.asarray(onehot), precision=lax.Precision.HIGHEST)

    x = layer_input.reshape(rows, width)
    g = output_gradient.reshape(rows, width)
    nvalid = jnp.clip(segment_length[0] - place * rows, 0, rows).astype(jnp.int32)

    def flags(section):
        core = lax.axis_index(AXES) % 2
        parts = [(place == section).astype(jnp.int32), nvalid, core, place]
        return jnp.stack([part.astype(jnp.int32) for part in parts])

    def hop(value, frm, to):
        route = [(d * count + frm, d * count + to) for d in range(pairs)]
        return lax.ppermute(value, AXES, route)

    kv, h1, new, *stash = advance(flags(0), gains, x, wa, None, None)
    for section in range(1, count):
        carry = hop(new, section - 1, section)
        new, *stash = advance(flags(section), gains, carry, wa, kv, stash)
    cs, hc, ckvq, upd, z, lse_two = stash

    quarter = new.shape[0] // count
    state_out = lax.dynamic_slice_in_dim(new, place * quarter, quarter, 0)
    for to in range(count - 1):
        got = hop(new[to * quarter : (to + 1) * quarter], count - 1, to)
        state_out = jnp.where(place == to, got, state_out)
    o, q, lse = token_forward(flags(0), t, h1, kv, ckvq, wa)
    wb, state_out, o = lax.optimization_barrier((wb, state_out, o))
    state_out = state_out.astype(F32)[None]

    x1, h2, act, dup, dx1, da, dq, dkv, dst, dbias, sums_mlp = block_part(
        flags(0), t, gains, x, g, o, q, lse, kv, ckvq, wb
    )

    early_args = (o, da, h1, dq, h2, dup, act, g)

    def only(active):
        parts = [active, nvalid, lax.axis_index(AXES) % 2]
        return jnp.stack([part.astype(jnp.int32) for part in parts])

    halves = early_grads(only(place < count - 1), share, (), *early_args)

    tie = lax.optimization_barrier
    early_orders, late_orders = orders_of(devices)
    back = None
    lam = state_cotangent.reshape(state_cotangent.shape[1:])
    lam, halves = tie((lam, halves))
    for section in reversed(range(count)):
        prev, back = retreat(flags(section), gains, lam, wa, kv, cs, ckvq, z, lse_two, dst, back, section > 0)
        if section == 0:
            break
        if section == count - 1:
            prev, halves = tie((prev, halves))
            lam = hop(prev, section, section - 1)
            halves = early_grads(only(place == count - 1), share, tuple(halves), *early_args)
            lam, halves = tie((lam, halves))
            if share % 32:
                whole = halves[0].reshape(devices, share, B_END)
                mine = lax.axis_index(AXES) % 2
                halves = [split_blocks(whole, 0, 1 - mine), split_blocks(whole, 0, mine)]
                cut = B_END // 2
                halves = [half[:, :, c : c + cut] for c in (0, cut) for half in halves]
        elif section == count - 2:
            prev, halves, x1 = tie((prev, halves, x1))
            early = [Stream(*halves[2 * n : 2 * n + 2], early_orders[n], devices) for n in range(2)]
            lam = hop(prev, section, section - 1)
            for stream in early:
                stream.move()
            layer_out = layer_output(x1, act, wb)
            layer_out, gots = tie((layer_out, [stream.got for stream in early]))
            for stream, got in zip(early, gots):
                stream.got = got
            step = Step(early)
            lam, sends = tie((lam, [stream.send for stream in early]))
            for stream, send in zip(early, sends):
                stream.send = send
                stream.move()
        else:
            prev = step.keep(prev)
            lam = hop(prev, section, section - 1)
            lam, keeps = tie((lam, [stream.keep for stream in early]))
            for stream, keep in zip(early, keeps):
                stream.keep = keep
    dz, dcs, dkv_two, sums_state = back

    tiles = [512 * n for n in range(4)]
    late_one = [("product", 0, (1, 512 * n)) for n in range(6)] + [("flip", 2, None)]
    late_two = [("sum", 0, ((1, 2), c)) for c in tiles] + [("product", 3, (4, c)) for c in tiles[:2]]
    def arrived(streams, others):
        gots, keeps, others = tie(([s.got for s in streams], [s.keep for s in streams], others))
        for stream, got, keep in zip(streams, gots, keeps):
            stream.got, stream.keep = got, keep
        return others

    def together(streams, other=None):
        sends = tie([stream.send for stream in streams])
        for stream, send in zip(streams, sends):
            stream.send = send
        result = other(jnp.minimum(jnp.abs(sends[0][0, 0, 0].astype(F32)), 0.0)) if other else ()
        for stream in streams:
            stream.move()
        return arrived(streams, result)

    prev, gots = tie((prev, [stream.got for stream in early]))
    for stream, got in zip(early, gots):
        stream.got = got
    split(early)
    switches = flags(0)
    switches, sends = tie((switches, [stream.send for stream in early]))
    for stream, send in zip(early, sends):
        stream.send = send
        stream.move()
    late = [
        late_grads(switches, share, late_one, hc, dcs, prev),
        late_grads(switches, share, late_two, h1, dkv, dkv_two, upd, dz),
    ]
    late = [Stream(*halves, order, devices) for halves, order in zip(arrived(early, late), late_orders)]
    for stream in late:
        stream.move()
    split(early)
    gots, sends, keeps = tie(
        ([s.got for s in late], [s.send for s in early], [s.keep for s in early])
    )
    for stream, got in zip(late, gots):
        stream.got = got
    for stream, send, keep in zip(early, sends, keeps):
        stream.send, stream.keep = send, keep
    split(late)
    x_grad, sums_attn = together(
        late + early, lambda zero: input_grad(gains + zero, x, dx1, dq, dkv, dkv_two, wa)
    )

    buckets = jnp.asarray(np.ascontiguousarray(onehot.T))
    dtable = jnp.dot(dbias, buckets, precision=lax.Precision.HIGHEST).reshape(devices, bias_local)
    dtable = jnp.pad(dtable, ((0, 0), (0, share - bias_local))).reshape(width)
    gate_grad = sums_state[1] * gate[0] * (1.0 - gate[0])
    vectors = jnp.stack([sums_attn[0], sums_mlp[0], sums_state[0], gate_grad, dtable], axis=1)
    vectors = jnp.pad(vectors, ((0, 0), (0, 123))).reshape(devices, share, 128)
    small = Few(vectors, sorted(late_orders[0]), devices)
    while late[0].order or small.order or small.send:
        running = [stream for stream in late + early if stream.order]
        if running:
            split(running)
        if small.send is None and small.order:
            small.split()
        together(running + ([small] if small.send else []))
    early = jnp.concatenate([stream.result() for stream in early], axis=1)
    one, two = [stream.result() for stream in late]
    vec = small.result()

    q_shard, out_shard, up_shard, down_shard = settle(early, devices)
    return (
        layer_out[None],
        state_out,
        x_grad[None],
        jnp.concatenate([q_shard, two[:, : 2 * width]], axis=1),
        one[:, : 2 * width],
        one[:, 2 * width : 3 * width],
        out_shard,
        two[:, 2 * width :],
        up_shard,
        down_shard,
        one[:, 3 * width :].T,
        vec[:, 0],
        vec[:, 1],
        vec[:, 2],
        vec[:, 3],
        vec[:bias_local, 4],
    )


def solution(mesh):
    return jax.shard_map(
        body,
        mesh=mesh,
        in_specs=(
            P("dp", "seq", None),
            P("dp"),
            P("dp", "seq", None),
            P("dp", None, None),
            P(AXES, None),
            P(AXES, None),
            P(AXES, None),
            P(AXES, None),
            P(AXES, None),
            P(AXES, None),
            P(AXES, None),
            P(None, AXES),
            P(AXES),
            P(AXES),
            P(AXES),
            P(AXES),
            P(AXES),
        ),
        out_specs=(
            P("dp", "seq", None),
            P("dp", "seq", None),
            P("dp", "seq", None),
            P(AXES, None),
            P(AXES, None),
            P(AXES, None),
            P(AXES, None),
            P(AXES, None),
            P(AXES, None),
            P(AXES, None),
            P(None, AXES),
            P(AXES),
            P(AXES),
            P(AXES),
            P(AXES),
            P(AXES),
        ),
        check_vma=False,
    )
```
